512 devices in a mesh: tile: 64 (over x, z, y_hi), mode: 8 (over y_lo, core).
Axes of the slice: x: 4, y: 8 (y_hi: 2, y_lo: 4; y = y_hi * 4 + y_lo), z: 8, core: 2. Of those that a mesh axis runs over, the one named last changes fastest.
Arguments:
- object_field: float32 [2, 16384, 768], P(None, 'tile'), may hold values from -5 to 5
- probe_modes: float32 [8, 2, 256, 256], P('mode'), may hold values from -5 to 5
- measured: bfloat16 [256, 256, 256], P('tile'), may hold values from 0.25 to 24
- offsets: int32 [256, 2], P('tile'), may hold values from 0 to 512, as said below
- counts: int32 [64], P('tile'), may hold values from 1 to 4, as said below
Outputs:
- object_grad: float32 [2, 16384, 768], P(None, ('tile', 'mode'))
- probe_grad: float32 [8, 2, 256, 256], P('mode')
The draws below stay inside these ranges and needn't reach their ends.
Inputs may be any that keep to these rules, and one draw needn't show every extreme that they name: `offsets`: row corners run from 0 to 256 and column corners from 0 to 512; a window's rows past its strip continue into the next strip, after the last strip into the first. Slot 0 of strip 0 has row 256 and column 512. A strip's live slots are its first counts[t]; some strip uses all 4.
All inputs are finite; a program needn't handle non-finite values.
Results may differ from the reference program's by a relative error of at most 0.0003.
Values sent between devices are 32-bit elements; how exact they have to be, the bound alone decides.
A program may use at most 64 MiB of HBM per device.

```python
import math
import jax
import jax.numpy as jnp
from jax import lax

PATCH = 256
CAP = 4
OW = 768
MODES = 8
STRIP = 256
OH = 16384
SLOTS = 256
N_TILE = 64


def draw_offsets(key, part):
    key = jax.random.fold_in(key, 11)
    first_key, second_key = jax.random.split(key)
    row_corner = jax.random.randint(first_key, (SLOTS, 1), 0, STRIP + 1)
    col_corner = jax.random.randint(second_key, (SLOTS, 1), 0, OW - PATCH + 1)
    leading = (jnp.arange(SLOTS) == 0)[:, None]
    row_corner = jnp.where(leading, STRIP, row_corner)
    col_corner = jnp.where(leading, OW - PATCH, col_corner)
    return jnp.concatenate([row_corner, col_corner], axis=1).astype(jnp.int32)


def draw_counts(key, part):
    key = jax.random.fold_in(key, 23)
    busy_key, light_key, pick_key = jax.random.split(key, 3)
    strips = SLOTS // CAP
    busy = jax.random.randint(busy_key, (strips,), 0, 10) < 3
    light = jnp.minimum(jax.random.randint(light_key, (strips,), 1, 3), CAP)
    result = jnp.where(busy, CAP, light)
    chosen = jax.random.randint(pick_key, (), 0, strips)
    result = jnp.where(jnp.arange(strips) == chosen, CAP, result)
    return result.astype(jnp.int32)


def block_scale(own_key, extent, cuts, low, high):
    level = 1.0
    for position, blocks in cuts:
        draws = jax.random.uniform(jax.random.fold_in(jax.random.fold_in(own_key, 6), position), (blocks,), jnp.float32, low / len(cuts), high / len(cuts))
        level = level * jnp.repeat(jnp.exp(draws), extent[position] // blocks).reshape((-1,) + (1,) * (len(extent) - 1 - position))
    return level


def scatter_about(key, dims, scale, limit, pieces=(), kind=jnp.bfloat16):
    values = jax.random.normal(key, dims, jnp.float32) * scale
    if len(pieces) > 0:
        values = block_scale(key, dims, pieces, -0.22, 0.18) * values
    return jnp.clip(values, min=-limit, max=limit).astype(kind)


def setup_inputs(seed: int = 0) -> dict:
    keys = jax.random.split(jax.random.key(seed), 6)
    object_field = scatter_about(keys[0], (2, OH, OW), 0.7, 5.0, ((1, 64),), jnp.float32)
    probe_modes = scatter_about(keys[1], (MODES, 2, PATCH, PATCH), 0.7, 5.0, ((0, 8),), jnp.float32)
    measured = jnp.clip(jnp.exp(math.log(24.0) - 4.564348 * jax.random.uniform(keys[2], (SLOTS, PATCH, PATCH), jnp.float32) ** block_scale(keys[2], (SLOTS, PATCH, PATCH), ((0, 64),), -0.2, 0.2)), 0.25, 24.0).astype(jnp.bfloat16)
    offsets = draw_offsets(jax.random.fold_in(keys[5], 71), 0)
    counts = draw_counts(jax.random.fold_in(keys[5], 71), 0)
    return dict(object_field=object_field, probe_modes=probe_modes, measured=measured, offsets=offsets, counts=counts)


def reference(object_field, probe_modes, measured, offsets, counts):
    whole_field = object_field[0] + 1j * object_field[1]
    probe_cplx = probe_modes[:, 0] + 1j * probe_modes[:, 1]
    total_rows = whole_field.shape[0]
    amplitudes = jnp.sqrt(measured.astype(jnp.float32)).reshape(N_TILE, CAP, PATCH, PATCH)
    corners = offsets.reshape(N_TILE, CAP, 2)

    def tile_step(probe_total, tile_index):
        row_index = (tile_index * STRIP + jnp.arange(2 * STRIP, dtype=jnp.int32)) % total_rows
        extended = jnp.take(whole_field, row_index, axis=0)
        placed = corners[tile_index]
        windows = jax.vmap(lambda p: lax.dynamic_slice(extended, (p[0], p[1]), (PATCH, PATCH)))(placed)
        exit_waves = probe_cplx[None] * windows[:, None]
        far_field = jnp.fft.fft2(exit_waves, norm='ortho')
        intensity = lax.optimization_barrier(jnp.sum(far_field.real ** 2 + far_field.imag ** 2, axis=1))
        live_mask = (jnp.arange(CAP, dtype=jnp.int32) < counts[tile_index]).astype(intensity.dtype)
        scaling = live_mask[:, None, None] * (1.0 - amplitudes[tile_index] / jnp.sqrt(jnp.maximum(intensity, 1.0)))
        returned = jnp.fft.ifft2(scaling[:, None] * far_field, norm='ortho')
        object_terms = lax.optimization_barrier(jnp.sum(jnp.conj(probe_cplx)[None] * returned, axis=1))
        probe_terms = lax.optimization_barrier(jnp.sum(jnp.conj(windows)[:, None] * returned, axis=0))
        accumulated = jnp.zeros_like(extended)
        for slot_index in range(CAP):
            corner = (placed[slot_index, 0], placed[slot_index, 1])
            current = lax.dynamic_slice(accumulated, corner, (PATCH, PATCH))
            accumulated = lax.dynamic_update_slice(accumulated, current + object_terms[slot_index], corner)
        return (probe_total + probe_terms, (accumulated[:STRIP], accumulated[STRIP:]))
    probe_total, (own_rows, spill_part) = lax.scan(tile_step, jnp.zeros_like(probe_cplx), jnp.arange(N_TILE, dtype=jnp.int32))
    combined = (own_rows + jnp.roll(spill_part, 1, axis=0)).reshape(total_rows, -1)
    object_grad = jnp.stack([combined.real, combined.imag]).astype(jnp.float32)
    probe_grad = jnp.stack([probe_total.real, probe_total.imag], axis=1).astype(jnp.float32)
    return (object_grad, probe_grad)
```

```python
import functools
import math

import jax
import jax.numpy as jnp
import numpy as np
from jax import lax
from jax.experimental import pallas as pl
from jax.experimental.pallas import tpu as pltpu
from jax.sharding import PartitionSpec as P

MESH = pl.DeviceIdType.MESH
F32 = jnp.float32
BF16 = jnp.bfloat16
VMEM = pl.BlockSpec(memory_space=pltpu.VMEM)
SMEM = pl.BlockSpec(memory_space=pltpu.SMEM)
ANY = pl.BlockSpec(memory_space=pl.ANY)
LIMIT = 56 * 1024 * 1024
PATCH = 256
STRIP = 256
WIDTH = 768
CAP = 4
CHIPS = 4
TALL, BROAD = PATCH + 8, PATCH + 128
PAIR = 2

HALO_CUTS = 4
SUM_CUTS = 4


def place():
    tile, mode = lax.axis_index("tile"), lax.axis_index("mode")
    return tile, mode, mode // 2, mode % 2


def ring_ends(tiles, tile, mode, chip, core):
    after = lax.rem(tile + 1, tiles)
    before = lax.rem(tile + tiles - 1, tiles)
    return dict(
        above=(jnp.where(chip < 3, tile, after), jnp.where(chip < 3, mode + 2, core)),
        below=(jnp.where(chip > 0, tile, after), jnp.where(chip > 0, mode - 2, core + 6)),
        to_below=(jnp.where(chip > 0, tile, before), jnp.where(chip > 0, mode - 2, core + 6)),
        to_above=(jnp.where(chip < 3, tile, before), jnp.where(chip < 3, mode + 2, core)),
    )


def greet(devices):
    barrier = pltpu.get_barrier_semaphore()
    for device in devices:
        pl.semaphore_signal(barrier, inc=1, device_id=device, device_id_type=MESH)
    pl.semaphore_wait(barrier, len(devices))


def remote(source, target, send_sem, recv_sem, device):
    return pltpu.make_async_remote_copy(
        src_ref=source, dst_ref=target, send_sem=send_sem, recv_sem=recv_sem, device_id=device, device_id_type=MESH
    )


def halo_kernel(tiles, object_ref, probe_ref, ext_ref, modes_ref, own_sem, probe_sem, probe_send, probe_recv,
                chain_send, chain_recv, pair_send, pair_recv):
    tile, mode, chip, core = place()
    sibling = (tile, mode + 1 - 2 * core)
    ends = ring_ends(tiles, tile, mode, chip, core)
    own_copy = pltpu.make_async_copy(object_ref, ext_ref.at[:, pl.ds(0, STRIP)], own_sem)
    own_copy.start()
    probe_copy = pltpu.make_async_copy(probe_ref.at[0], modes_ref.at[core], probe_sem)
    probe_copy.start()
    greet([ends["above"], ends["below"], ends["to_above"], ends["to_below"], sibling])
    swap = remote(probe_ref.at[0], modes_ref.at[core], probe_send, probe_recv, sibling)
    swap.start()
    own_copy.wait()

    depth = STRIP // 4 // HALO_CUTS
    targets = (ends["to_below"], ends["to_above"])
    passes_on = (chip > 0, chip < 3)

    def rows(way, cut):
        return (2 * way + core) * (STRIP // 4) + cut * depth

    def chain(way, cut, base):
        row = rows(way, cut)
        return remote(
            ext_ref.at[:, pl.ds(base + row, depth)],
            ext_ref.at[:, pl.ds(STRIP + row, depth)],
            chain_send.at[way, cut],
            chain_recv.at[way, cut],
            targets[way],
        )

    def across(way, cut):
        block = ext_ref.at[:, pl.ds(STRIP + rows(way, cut), depth)]
        return remote(block, block, pair_send.at[way, cut], pair_recv.at[way, cut], sibling)

    for way in range(2):
        @pl.when(jnp.logical_not(passes_on[way]))
        def _():
            for cut in range(HALO_CUTS):
                chain(way, cut, 0).start()

    for cut in range(HALO_CUTS):
        for way in range(2):
            chain(way, cut, 0).wait_recv()
            @pl.when(passes_on[way])
            def _():
                chain(way, cut, STRIP).start()
            across(way, cut).start()

    for cut in range(HALO_CUTS):
        for way in range(2):
            chain(way, cut, 0).wait_send()
            across(way, cut).wait_send()
    for cut in range(HALO_CUTS):
        for way in range(2):
            sent = (2 * way + 1 - core) * (STRIP // 4) + cut * depth
            block = ext_ref.at[:, pl.ds(STRIP + sent, depth)]
            remote(block, block, pair_send.at[way, cut], pair_recv.at[way, cut], sibling).wait_recv()
    swap.wait()
    probe_copy.wait()


def halo(tiles, object_field, probe_modes):
    return pl.pallas_call(
        functools.partial(halo_kernel, tiles),
        out_shape=(
            jax.ShapeDtypeStruct((2, 2 * STRIP, WIDTH), F32),
            jax.ShapeDtypeStruct((PAIR, 2, PATCH, PATCH), F32),
        ),
        in_specs=[ANY, VMEM],
        out_specs=(VMEM, VMEM),
        scratch_shapes=[
            pltpu.SemaphoreType.DMA,
            pltpu.SemaphoreType.DMA,
            pltpu.SemaphoreType.DMA,
            pltpu.SemaphoreType.DMA,
            pltpu.SemaphoreType.DMA((2, HALO_CUTS)),
            pltpu.SemaphoreType.DMA((2, HALO_CUTS)),
            pltpu.SemaphoreType.DMA((2, HALO_CUTS)),
            pltpu.SemaphoreType.DMA((2, HALO_CUTS)),
        ],
        compiler_params=pltpu.CompilerParams(collective_id=0, has_side_effects=True, vmem_limit_bytes=LIMIT),
        name="halo",
    )(object_field, probe_modes)


def split(value):
    high = value.astype(BF16)
    return high, (value - high.astype(F32)).astype(BF16)


def dft_tables():
    index = np.arange(PATCH)
    angle = 2.0 * math.pi * ((index[:, None] * index[None, :]) % PATCH) / PATCH
    cos, sin = np.cos(angle) / math.sqrt(PATCH), np.sin(angle) / math.sqrt(PATCH)

    def parts(block):
        high = block.astype(jnp.bfloat16)
        low = (block - high.astype(np.float64)).astype(jnp.bfloat16)
        return high, low

    tables = []
    for sine in (-sin, sin):
        high, low = parts(np.block([[cos, -sine], [sine, cos]]))
        tables.append(np.concatenate([high, high, low], axis=1))
        high, low = parts(np.block([[cos, sine], [-sine, cos]]))
        tables.append(np.concatenate([high, high, low], axis=0))
    return tables


def transform(real, imag, left_ref, right_ref):
    high, low = split(jnp.concatenate([real, imag], axis=0))
    mid = jnp.dot(left_ref[...], jnp.concatenate([high, low, high], axis=0), preferred_element_type=F32)
    high, low = split(jnp.concatenate([mid[:PATCH], mid[PATCH:]], axis=1))
    out = jnp.dot(jnp.concatenate([high, low, high], axis=1), right_ref[...], preferred_element_type=F32)
    return out[:, :PATCH], out[:, PATCH:]


def corner(offsets_ref, slot):
    row, column = offsets_ref[slot, 0], offsets_ref[slot, 1]
    top = jnp.minimum(row // 8, (2 * STRIP - TALL) // 8) * 8
    left = jnp.minimum(column // 128, (WIDTH - BROAD) // 128) * 128
    return pl.ds(pl.multiple_of(top, 8), TALL), pl.ds(pl.multiple_of(left, 128), BROAD), row - top, column - left


def forward_kernel(ext_ref, modes_ref, offsets_ref, left_ref, right_ref, windows_ref, far_ref, power_ref):
    core = lax.axis_index("mode") % 2
    for local in range(2):
        rows, columns, down, right = corner(offsets_ref, 2 * core + local)
        window = []
        for part in range(2):
            block = pltpu.roll(ext_ref[part, rows, columns], lax.rem(BROAD - right, BROAD), 1)[:, :PATCH]
            block = pltpu.roll(block, lax.rem(TALL - down, TALL), 0)[:PATCH]
            windows_ref[local, part] = block
            window.append(block)
        for pair in range(PAIR):
            mode_real, mode_imag = modes_ref[pair, 0], modes_ref[pair, 1]
            far_real, far_imag = transform(
                mode_real * window[0] - mode_imag * window[1],
                mode_real * window[1] + mode_imag * window[0],
                left_ref,
                right_ref,
            )
            far_ref[local, pair, 0] = far_real
            far_ref[local, pair, 1] = far_imag
            power = far_real * far_real + far_imag * far_imag
            if pair == 0:
                power_ref[local] = power
            else:
                power_ref[local] += power


def forward(ext, modes, offsets, left, right):
    return pl.pallas_call(
        forward_kernel,
        out_shape=(
            jax.ShapeDtypeStruct((2, 2, PATCH, PATCH), F32),
            jax.ShapeDtypeStruct((2, PAIR, 2, PATCH, PATCH), F32),
            jax.ShapeDtypeStruct((2, PATCH, PATCH), F32),
        ),
        in_specs=[VMEM, VMEM, SMEM, VMEM, VMEM],
        out_specs=(VMEM, VMEM, VMEM),
        compiler_params=pltpu.CompilerParams(vmem_limit_bytes=LIMIT),
        name="forward",
    )(ext, modes, offsets, left, right)


def sum_kernel(power_ref, total_ref, staged, arrived, send_sem, recv_sem):
    tile, mode, chip, core = place()
    lower, upper = (tile, mode - 2), (tile, mode + 2)
    has_lower, has_upper = chip > 0, chip < CHIPS - 1
    barrier = pltpu.get_barrier_semaphore()
    for there, device in ((has_lower, lower), (has_upper, upper)):
        @pl.when(there)
        def _():
            pl.semaphore_signal(barrier, inc=1, device_id=device, device_id_type=MESH)
    pl.semaphore_wait(barrier, has_lower.astype(jnp.int32) + has_upper.astype(jnp.int32))

    depth = 2 * PATCH // SUM_CUTS

    def block(cut):
        return pl.ds(cut * depth, depth)

    ways = ((has_lower, has_upper, upper), (has_upper, has_lower, lower))

    def hop(way, cut, source):
        return remote(
            source.at[block(cut)], arrived.at[way, block(cut)], send_sem.at[way, cut], recv_sem.at[way, cut], ways[way][2]
        )

    for way, (hears, sends, _) in enumerate(ways):
        @pl.when(jnp.logical_not(hears))
        def _():
            for cut in range(SUM_CUTS):
                hop(way, cut, power_ref).start()

    for cut in range(SUM_CUTS):
        for way, (hears, sends, _) in enumerate(ways):
            @pl.when(hears)
            def _():
                hop(way, cut, power_ref).wait_recv()

            @pl.when(jnp.logical_and(hears, sends))
            def _():
                staged[way, block(cut)] = power_ref[block(cut)] + arrived[way, block(cut)]
                hop(way, cut, staged.at[way]).start()
        rows = block(cut)

        @pl.when(jnp.logical_not(has_lower))
        def _():
            total_ref[rows] = power_ref[rows] + arrived[1, rows]

        @pl.when(jnp.logical_not(has_upper))
        def _():
            total_ref[rows] = power_ref[rows] + arrived[0, rows]

        @pl.when(jnp.logical_and(has_lower, has_upper))
        def _():
            total_ref[rows] = power_ref[rows] + (arrived[0, rows] + arrived[1, rows])

    for way, (hears, sends, _) in enumerate(ways):
        @pl.when(sends)
        def _():
            for cut in range(SUM_CUTS):
                hop(way, cut, power_ref).wait_send()


def sum_power(power):
    rows = 2 * PATCH
    return pl.pallas_call(
        sum_kernel,
        out_shape=jax.ShapeDtypeStruct((rows, PATCH), F32),
        in_specs=[VMEM],
        out_specs=VMEM,
        scratch_shapes=[
            pltpu.VMEM((2, rows, PATCH), F32),
            pltpu.VMEM((2, rows, PATCH), F32),
            pltpu.SemaphoreType.DMA((2, SUM_CUTS)),
            pltpu.SemaphoreType.DMA((2, SUM_CUTS)),
        ],
        compiler_params=pltpu.CompilerParams(collective_id=1, has_side_effects=True, vmem_limit_bytes=LIMIT),
        name="sum_power",
    )(power.reshape(rows, PATCH)).reshape(2, PATCH, PATCH)


def back_kernel(total_ref, far_ref, windows_ref, modes_ref, measured_ref, offsets_ref, counts_ref, left_ref, right_ref,
                acc_ref, probe_ref):
    core = lax.axis_index("mode") % 2
    acc_ref[...] = jnp.zeros_like(acc_ref)
    for local in range(2):
        slot = 2 * core + local
        amplitude = jnp.sqrt(measured_ref[slot].astype(F32))
        live = (slot < counts_ref[0]).astype(F32)
        scaling = live * (1.0 - amplitude / jnp.sqrt(jnp.maximum(total_ref[local], 1.0)))
        win_real, win_imag = windows_ref[local, 0], windows_ref[local, 1]
        term_real = term_imag = None
        for pair in range(PAIR):
            back_real, back_imag = transform(
                scaling * far_ref[local, pair, 0], scaling * far_ref[local, pair, 1], left_ref, right_ref
            )
            mode_real, mode_imag = modes_ref[pair, 0], modes_ref[pair, 1]
            grad_real = mode_real * back_real + mode_imag * back_imag
            grad_imag = mode_real * back_imag - mode_imag * back_real
            term_real = grad_real if term_real is None else term_real + grad_real
            term_imag = grad_imag if term_imag is None else term_imag + grad_imag
            probe_real = win_real * back_real + win_imag * back_imag
            probe_imag = win_real * back_imag - win_imag * back_real
            if local == 0:
                probe_ref[pair, 0] = probe_real
                probe_ref[pair, 1] = probe_imag
            else:
                probe_ref[pair, 0] += probe_real
                probe_ref[pair, 1] += probe_imag
        rows, columns, down, right = corner(offsets_ref, slot)
        for part, term in enumerate((term_real, term_imag)):
            term = jnp.concatenate([term, jnp.zeros((TALL - PATCH, PATCH), F32)], axis=0)
            term = jnp.concatenate([pltpu.roll(term, down, 0), jnp.zeros((TALL, BROAD - PATCH), F32)], axis=1)
            acc_ref[part, rows, columns] += pltpu.roll(term, right, 1)


def back(total, far, windows, modes, measured, offsets, counts, left, right):
    return pl.pallas_call(
        back_kernel,
        out_shape=(
            jax.ShapeDtypeStruct((2, 2 * STRIP, WIDTH), F32),
            jax.ShapeDtypeStruct((PAIR, 2, PATCH, PATCH), F32),
        ),
        in_specs=[VMEM, VMEM, VMEM, VMEM, VMEM, SMEM, SMEM, VMEM, VMEM],
        out_specs=(VMEM, VMEM),
        compiler_params=pltpu.CompilerParams(vmem_limit_bytes=LIMIT),
        name="back",
    )(total, far, windows, modes, measured, offsets, counts, left, right)


def gather_kernel(tiles, grid_x, grid_z, acc_ref, terms_ref, object_ref, probe_ref, pair_buf, up_out, up_in, down_out,
                  down_in, probe_buf, mine, x_in, z_in, pair_send, pair_recv, up_send, up_recv, down_send, down_recv,
                  probe_send, probe_recv, x_send, x_recv, z_send, z_recv, h_send, h_recv, zg_send, zg_recv, xg_send,
                  xg_recv):
    tile, mode, chip, core = place()
    sibling = (tile, mode + 1 - 2 * core)
    after = lax.rem(tile + 1, tiles)
    before = lax.rem(tile + tiles - 1, tiles)
    to_up = (jnp.where(chip < 3, tile, after), jnp.where(chip < 3, mode + 2, core))
    from_up = (jnp.where(chip > 0, tile, before), jnp.where(chip > 0, mode - 2, core + 6))
    to_down = (jnp.where(chip > 0, tile, after), jnp.where(chip > 0, mode - 2, core + 6))
    from_down = (jnp.where(chip < 3, tile, before), jnp.where(chip < 3, mode + 2, core))

    high, plane = tile % 2, tile // 2
    at_z, at_x = plane % grid_z, plane // grid_z

    def at(x, z, h):
        return ((x * grid_z + z) * 2 + h, mode)

    x_peers = [lax.rem(at_x + step, grid_x) for step in range(1, grid_x)]
    z_peers = [lax.rem(at_z + step, grid_z) for step in range(1, grid_z)]
    x_ids = [at(peer, at_z, high) for peer in x_peers]
    z_ids = [at(at_x, peer, high) for peer in z_peers]
    h_id = at(at_x, at_z, 1 - high)
    greet([to_up, from_up, to_down, from_down, sibling, h_id] + x_ids + z_ids)

    probe_pair = remote(terms_ref.at[1 - core], probe_buf, probe_send, probe_recv, sibling)
    probe_pair.start()

    def pair_copy(block):
        return remote(
            acc_ref.at[:, 2 * block + 1 - core], pair_buf.at[:, block], pair_send.at[block], pair_recv.at[block], sibling
        )

    pair_order = (4, 7, 5, 6, 3, 0, 2, 1)
    for block in pair_order:
        pair_copy(block).start()

    ready = set()

    def part(block):
        if block not in ready:
            ready.add(block)
            pair_copy(block).wait()
            pair_buf[:, block] += acc_ref[:, 2 * block + core]
        return pair_buf[:, block]

    depth_x = 2 * PATCH // grid_x
    depth_z = depth_x // grid_z
    probe_pair.wait()
    mine[...] = probe_buf[...] + terms_ref[core]

    def x_copy(step):
        peer = x_peers[step]
        return remote(
            mine.at[pl.ds(peer * depth_x, depth_x)], x_in.at[step], x_send.at[step], x_recv.at[step], x_ids[step]
        )

    for step in range(grid_x - 1):
        x_copy(step).start()

    def up_copy(item):
        return remote(up_out.at[item], up_in.at[item], up_send.at[item], up_recv.at[item], to_up)

    def down_copy(item):
        return remote(down_out.at[item], down_in.at[item], down_send.at[item], down_recv.at[item], to_down)

    chains = (
        (up_copy, up_out, up_in, chip, (4, 5, 3, 2, 1)),
        (down_copy, down_out, down_in, CHIPS - 1 - chip, (7, 6, 0, 1, 2)),
    )

    for block in pair_order:
        part(block)

    def advance(way, item):
        copy, out, arrived, rank, blocks = chains[way]
        block = blocks[item]
        if item < 2:
            @pl.when(rank == 0)
            def _():
                out[item] = pair_buf[:, block]

            @pl.when(rank > 0)
            def _():
                copy(item).wait_recv()
                out[item] = pair_buf[:, block] + arrived[item]

            copy(item).start()
        else:
            last = 5 - item
            if item < 4:
                @pl.when(rank == 0)
                def _():
                    out[item] = pair_buf[:, block]
                    copy(item).start()

                @pl.when(jnp.logical_and(rank > 0, rank < last))
                def _():
                    copy(item).wait_recv()
                    out[item] = pair_buf[:, block] + arrived[item]
                    copy(item).start()
            else:
                @pl.when(rank == 0)
                def _():
                    copy(1).wait_recv()
                    out[item] = pair_buf[:, block] + arrived[1]
                    copy(item).start()

    for item in range(4):
        advance(0, item)
        advance(1, item)

    for step in range(grid_x - 1):
        x_copy(step).wait()
    own_x = pl.ds(at_x * depth_x, depth_x)
    total = mine[own_x]
    for step in range(grid_x - 1):
        total = total + x_in[step]
    mine[own_x] = total

    def z_copy(step):
        peer = z_peers[step]
        return remote(
            mine.at[pl.ds(at_x * depth_x + peer * depth_z, depth_z)],
            z_in.at[step],
            z_send.at[step],
            z_recv.at[step],
            z_ids[step],
        )

    for step in range(grid_z - 1):
        z_copy(step).start()
    for step in range(grid_z - 1):
        z_copy(step).wait()
    own_z = pl.ds(at_x * depth_x + at_z * depth_z, depth_z)
    total = mine[own_z]
    for step in range(grid_z - 1):
        total = total + z_in[step]
    mine[own_z] = total

    h_copy = remote(mine.at[own_z], z_in.at[grid_z - 1], h_send, h_recv, h_id)
    h_copy.start()
    for way in range(2):
        advance(way, 4)
    h_copy.wait()
    probe_ref[own_z] = mine[own_z] + z_in[grid_z - 1]

    def z_back(step, owner):
        rows = pl.ds(at_x * depth_x + owner * depth_z, depth_z)
        return remote(probe_ref.at[rows], probe_ref.at[rows], zg_send.at[step], zg_recv.at[step], z_ids[step])

    for step in range(grid_z - 1):
        z_back(step, at_z).start()
    for step in range(grid_z - 1):
        z_back(step, at_z).wait_send()
        sender = lax.rem(at_z + grid_z - step - 1, grid_z)
        z_back(step, sender).wait_recv()

    def x_back(step, owner):
        rows = pl.ds(owner * depth_x, depth_x)
        return remote(probe_ref.at[rows], probe_ref.at[rows], xg_send.at[step], xg_recv.at[step], x_ids[step])

    for step in range(grid_x - 1):
        x_back(step, at_x).start()

    for chip_at in range(CHIPS):
        @pl.when(chip == chip_at)
        def _():
            result = pair_buf[:, chip_at]
            for way in range(2):
                copy, out, arrived, rank, blocks = chains[way]
                here = chip_at if way == 0 else CHIPS - 1 - chip_at
                if here == 0:
                    copy(0).wait_recv()
                    result = result + arrived[0]
                else:
                    copy(5 - here).wait_recv()
                    result = result + arrived[5 - here]
            object_ref[...] = result

    for way in range(2):
        copy, out, arrived, rank, blocks = chains[way]
        for item in range(5):
            if item < 2:
                copy(item).wait_send()
            else:
                @pl.when(rank < 5 - item)
                def _():
                    copy(item).wait_send()

    for step in range(grid_x - 1):
        x_back(step, at_x).wait_send()
        sender = lax.rem(at_x + grid_x - step - 1, grid_x)
        x_back(step, sender).wait_recv()


def gather(tiles, grid_x, grid_z, acc, terms):
    rows = 2 * PATCH
    depth_x = rows // grid_x
    depth_z = depth_x // grid_z
    block = (2, 32, WIDTH)
    dma = pltpu.SemaphoreType.DMA
    object_rows, probe = pl.pallas_call(
        functools.partial(gather_kernel, tiles, grid_x, grid_z),
        out_shape=(jax.ShapeDtypeStruct(block, F32), jax.ShapeDtypeStruct((rows, PATCH), F32)),
        in_specs=[VMEM, VMEM],
        out_specs=(VMEM, VMEM),
        scratch_shapes=[
            pltpu.VMEM((2, 8, 32, WIDTH), F32),
            pltpu.VMEM((5,) + block, F32),
            pltpu.VMEM((5,) + block, F32),
            pltpu.VMEM((5,) + block, F32),
            pltpu.VMEM((5,) + block, F32),
            pltpu.VMEM((rows, PATCH), F32),
            pltpu.VMEM((rows, PATCH), F32),
            pltpu.VMEM((max(grid_x - 1, 1), depth_x, PATCH), F32),
            pltpu.VMEM((grid_z, depth_z, PATCH), F32),
            dma((8,)), dma((8,)),
            dma((5,)), dma((5,)), dma((5,)), dma((5,)),
            dma, dma,
            dma((max(grid_x - 1, 1),)), dma((max(grid_x - 1, 1),)),
            dma((grid_z,)), dma((grid_z,)),
            dma, dma,
            dma((grid_z,)), dma((grid_z,)),
            dma((max(grid_x - 1, 1),)), dma((max(grid_x - 1, 1),)),
        ],
        compiler_params=pltpu.CompilerParams(collective_id=2, has_side_effects=True, vmem_limit_bytes=LIMIT),
        name="gather",
    )(acc.reshape(2, 16, 32, WIDTH), terms.reshape(PAIR, rows, PATCH))
    return object_rows, probe.reshape(1, 2, PATCH, PATCH)


def solution(mesh):
    tiles = mesh.shape["tile"]
    grid_x = 4 if tiles == 64 else 2
    grid_z = tiles // 2 // grid_x
    left_forward, right_forward, left_back, right_back = dft_tables()

    def body(object_field, probe_modes, measured, offsets, counts):
        ext, modes = halo(tiles, object_field, probe_modes)
        windows, far, power = forward(ext, modes, offsets, jnp.asarray(left_forward), jnp.asarray(right_forward))
        total = sum_power(power)
        acc, terms = back(
            total, far, windows, modes, measured, offsets, counts, jnp.asarray(left_back), jnp.asarray(right_back)
        )
        return gather(tiles, grid_x, grid_z, acc, terms)

    return jax.shard_map(
        body,
        mesh=mesh,
        in_specs=(
            P(None, "tile", None),
            P("mode", None, None, None),
            P("tile", None, None),
            P("tile", None),
            P("tile"),
        ),
        out_specs=(P(None, ("tile", "mode"), None), P("mode", None, None, None)),
        check_vma=False,
    )
```

```python
import functools
import math

import jax
import jax.numpy as jnp
import numpy as np
from jax import lax
from jax.experimental import pallas as pl
from jax.experimental.pallas import tpu as pltpu
from jax.sharding import PartitionSpec as P

MESH = pl.DeviceIdType.MESH
F32 = jnp.float32
BF16 = jnp.bfloat16
VMEM = pl.BlockSpec(memory_space=pltpu.VMEM)
SMEM = pl.BlockSpec(memory_space=pltpu.SMEM)
ANY = pl.BlockSpec(memory_space=pl.ANY)
LIMIT = 56 * 1024 * 1024
PATCH = 256
STRIP = 256
WIDTH = 768
CAP = 4
CHIPS = 4
TALL, BROAD = PATCH + 8, PATCH + 128
PAIR = 2

HALO_CUTS = 8
SUM_CUTS = 16
LATENCY = 2.3


def place():
    tile, mode = lax.axis_index("tile"), lax.axis_index("mode")
    return tile, mode, mode // 2, mode % 2


def ring_ends(tiles, tile, mode, chip, core):
    after = lax.rem(tile + 1, tiles)
    before = lax.rem(tile + tiles - 1, tiles)
    return dict(
        above=(jnp.where(chip < 3, tile, after), jnp.where(chip < 3, mode + 2, core)),
        below=(jnp.where(chip > 0, tile, after), jnp.where(chip > 0, mode - 2, core + 6)),
        to_below=(jnp.where(chip > 0, tile, before), jnp.where(chip > 0, mode - 2, core + 6)),
        to_above=(jnp.where(chip < 3, tile, before), jnp.where(chip < 3, mode + 2, core)),
    )


def greet(devices):
    barrier = pltpu.get_barrier_semaphore()
    for device in devices:
        pl.semaphore_signal(barrier, inc=1, device_id=device, device_id_type=MESH)
    pl.semaphore_wait(barrier, len(devices))


def remote(source, target, send_sem, recv_sem, device):
    return pltpu.make_async_remote_copy(
        src_ref=source, dst_ref=target, send_sem=send_sem, recv_sem=recv_sem, device_id=device, device_id_type=MESH
    )


def halo_kernel(tiles, object_ref, probe_ref, ext_ref, modes_ref, own_sem, probe_sem, probe_send, probe_recv,
                chain_send, chain_recv, pair_send, pair_recv):
    tile, mode, chip, core = place()
    sibling = (tile, mode + 1 - 2 * core)
    ends = ring_ends(tiles, tile, mode, chip, core)
    own_copy = pltpu.make_async_copy(object_ref, ext_ref.at[:, pl.ds(0, STRIP)], own_sem)
    own_copy.start()
    probe_copy = pltpu.make_async_copy(probe_ref.at[0], modes_ref.at[core], probe_sem)
    probe_copy.start()
    greet([ends["above"], ends["below"], ends["to_above"], ends["to_below"], sibling])
    swap = remote(probe_ref.at[0], modes_ref.at[core], probe_send, probe_recv, sibling)
    swap.start()
    own_copy.wait()

    depth = STRIP // 4 // HALO_CUTS
    targets = (ends["to_below"], ends["to_above"])
    passes_on = (chip > 0, chip < 3)

    def rows(way, cut):
        return (2 * way + core) * (STRIP // 4) + cut * depth

    def chain(way, cut, base):
        row = rows(way, cut)
        return remote(
            ext_ref.at[:, pl.ds(base + row, depth)],
            ext_ref.at[:, pl.ds(STRIP + row, depth)],
            chain_send.at[way, cut],
            chain_recv.at[way, cut],
            targets[way],
        )

    def across(way, cut):
        block = ext_ref.at[:, pl.ds(STRIP + rows(way, cut), depth)]
        return remote(block, block, pair_send.at[way, cut], pair_recv.at[way, cut], sibling)

    for way in range(2):
        @pl.when(jnp.logical_not(passes_on[way]))
        def _():
            for cut in range(HALO_CUTS):
                chain(way, cut, 0).start()

    for here in range(CHIPS):
        @pl.when(chip == here)
        def _():
            step = 8.0 / HALO_CUTS
            events = []
            for way, rank in ((0, CHIPS - 1 - here), (1, here)):
                for cut in range(HALO_CUTS):
                    events.append(((rank + 1) * (step + LATENCY) + cut * step, way, cut, rank < CHIPS - 1))
            for _, way, cut, forwards in sorted(events):
                chain(way, cut, 0).wait_recv()
                if forwards:
                    chain(way, cut, STRIP).start()
                across(way, cut).start()

    for cut in range(HALO_CUTS):
        for way in range(2):
            chain(way, cut, 0).wait_send()
            across(way, cut).wait_send()
    for cut in range(HALO_CUTS):
        for way in range(2):
            sent = (2 * way + 1 - core) * (STRIP // 4) + cut * depth
            block = ext_ref.at[:, pl.ds(STRIP + sent, depth)]
            remote(block, block, pair_send.at[way, cut], pair_recv.at[way, cut], sibling).wait_recv()
    swap.wait()
    probe_copy.wait()


def halo(tiles, object_field, probe_modes):
    return pl.pallas_call(
        functools.partial(halo_kernel, tiles),
        out_shape=(
            jax.ShapeDtypeStruct((2, 2 * STRIP, WIDTH), F32),
            jax.ShapeDtypeStruct((PAIR, 2, PATCH, PATCH), F32),
        ),
        in_specs=[ANY, VMEM],
        out_specs=(VMEM, VMEM),
        scratch_shapes=[
            pltpu.SemaphoreType.DMA,
            pltpu.SemaphoreType.DMA,
            pltpu.SemaphoreType.DMA,
            pltpu.SemaphoreType.DMA,
            pltpu.SemaphoreType.DMA((2, HALO_CUTS)),
            pltpu.SemaphoreType.DMA((2, HALO_CUTS)),
            pltpu.SemaphoreType.DMA((2, HALO_CUTS)),
            pltpu.SemaphoreType.DMA((2, HALO_CUTS)),
        ],
        compiler_params=pltpu.CompilerParams(collective_id=0, has_side_effects=True, vmem_limit_bytes=LIMIT),
        name="halo",
    )(object_field, probe_modes)


def split(value):
    high = value.astype(BF16)
    return high, (value - high.astype(F32)).astype(BF16)


def dft_tables():
    index = np.arange(PATCH)
    angle = 2.0 * math.pi * ((index[:, None] * index[None, :]) % PATCH) / PATCH
    cos, sin = np.cos(angle) / math.sqrt(PATCH), np.sin(angle) / math.sqrt(PATCH)

    def parts(block):
        high = block.astype(jnp.bfloat16)
        low = (block - high.astype(np.float64)).astype(jnp.bfloat16)
        return high, low

    tables = []
    for sine in (-sin, sin):
        high, low = parts(np.block([[cos, -sine], [sine, cos]]))
        tables.append(np.concatenate([high, high, low], axis=1))
        high, low = parts(np.block([[cos, sine], [-sine, cos]]))
        tables.append(np.concatenate([high, high, low], axis=0))
    return tables


def transform(real, imag, left_ref, right_ref):
    high, low = split(jnp.concatenate([real, imag], axis=0))
    mid = jnp.dot(left_ref[...], jnp.concatenate([high, low, high], axis=0), preferred_element_type=F32)
    high, low = split(jnp.concatenate([mid[:PATCH], mid[PATCH:]], axis=1))
    out = jnp.dot(jnp.concatenate([high, low, high], axis=1), right_ref[...], preferred_element_type=F32)
    return out[:, :PATCH], out[:, PATCH:]


def corner(offsets_ref, slot):
    row, column = offsets_ref[slot, 0], offsets_ref[slot, 1]
    top = jnp.minimum(row // 8, (2 * STRIP - TALL) // 8) * 8
    left = jnp.minimum(column // 128, (WIDTH - BROAD) // 128) * 128
    return pl.ds(pl.multiple_of(top, 8), TALL), pl.ds(pl.multiple_of(left, 128), BROAD), row - top, column - left


def forward_kernel(ext_ref, modes_ref, offsets_ref, left_ref, right_ref, windows_ref, far_ref, power_ref):
    core = lax.axis_index("mode") % 2
    for local in range(2):
        rows, columns, down, right = corner(offsets_ref, 2 * core + local)
        window = []
        for part in range(2):
            block = pltpu.roll(ext_ref[part, rows, columns], lax.rem(BROAD - right, BROAD), 1)[:, :PATCH]
            block = pltpu.roll(block, lax.rem(TALL - down, TALL), 0)[:PATCH]
            windows_ref[local, part] = block
            window.append(block)
        for pair in range(PAIR):
            mode_real, mode_imag = modes_ref[pair, 0], modes_ref[pair, 1]
            far_real, far_imag = transform(
                mode_real * window[0] - mode_imag * window[1],
                mode_real * window[1] + mode_imag * window[0],
                left_ref,
                right_ref,
            )
            far_ref[local, pair, 0] = far_real
            far_ref[local, pair, 1] = far_imag
            power = far_real * far_real + far_imag * far_imag
            if pair == 0:
                power_ref[local] = power
            else:
                power_ref[local] += power


def forward(ext, modes, offsets, left, right):
    return pl.pallas_call(
        forward_kernel,
        out_shape=(
            jax.ShapeDtypeStruct((2, 2, PATCH, PATCH), F32),
            jax.ShapeDtypeStruct((2, PAIR, 2, PATCH, PATCH), F32),
            jax.ShapeDtypeStruct((2, PATCH, PATCH), F32),
        ),
        in_specs=[VMEM, VMEM, SMEM, VMEM, VMEM],
        out_specs=(VMEM, VMEM, VMEM),
        compiler_params=pltpu.CompilerParams(vmem_limit_bytes=LIMIT),
        name="forward",
    )(ext, modes, offsets, left, right)


def sum_kernel(power_ref, total_ref, staged, arrived, send_sem, recv_sem):
    tile, mode, chip, core = place()
    lower, upper = (tile, mode - 2), (tile, mode + 2)
    has_lower, has_upper = chip > 0, chip < CHIPS - 1
    barrier = pltpu.get_barrier_semaphore()
    for there, device in ((has_lower, lower), (has_upper, upper)):
        @pl.when(there)
        def _():
            pl.semaphore_signal(barrier, inc=1, device_id=device, device_id_type=MESH)
    pl.semaphore_wait(barrier, has_lower.astype(jnp.int32) + has_upper.astype(jnp.int32))

    depth = 2 * PATCH // SUM_CUTS

    def block(cut):
        return pl.ds(cut * depth, depth)

    ways = ((has_lower, has_upper, upper), (has_upper, has_lower, lower))

    def hop(way, cut, source):
        return remote(
            source.at[block(cut)], arrived.at[way, block(cut)], send_sem.at[way, cut], recv_sem.at[way, cut], ways[way][2]
        )

    for way, (hears, sends, _) in enumerate(ways):
        @pl.when(jnp.logical_not(hears))
        def _():
            for cut in range(SUM_CUTS):
                hop(way, cut, power_ref).start()

    for here in range(CHIPS):
        @pl.when(chip == here)
        def _():
            step = 10.5 / SUM_CUTS
            events = []
            for way, rank in ((0, here), (1, CHIPS - 1 - here)):
                if rank > 0:
                    for cut in range(SUM_CUTS):
                        events.append((rank * (step + LATENCY) + cut * step, way, cut, rank < CHIPS - 1))
            seen = [0] * SUM_CUTS
            for _, way, cut, forwards in sorted(events):
                rows = block(cut)
                hop(way, cut, power_ref).wait_recv()
                if forwards:
                    staged[way, rows] = power_ref[rows] + arrived[way, rows]
                    hop(way, cut, staged.at[way]).start()
                seen[cut] += 1
                if seen[cut] == 1 + (0 < here < CHIPS - 1):
                    if 0 < here < CHIPS - 1:
                        total_ref[rows] = power_ref[rows] + (arrived[0, rows] + arrived[1, rows])
                    else:
                        total_ref[rows] = power_ref[rows] + arrived[way, rows]

    for way, (hears, sends, _) in enumerate(ways):
        @pl.when(sends)
        def _():
            for cut in range(SUM_CUTS):
                hop(way, cut, power_ref).wait_send()


def sum_power(power):
    rows = 2 * PATCH
    return pl.pallas_call(
        sum_kernel,
        out_shape=jax.ShapeDtypeStruct((rows, PATCH), F32),
        in_specs=[VMEM],
        out_specs=VMEM,
        scratch_shapes=[
            pltpu.VMEM((2, rows, PATCH), F32),
            pltpu.VMEM((2, rows, PATCH), F32),
            pltpu.SemaphoreType.DMA((2, SUM_CUTS)),
            pltpu.SemaphoreType.DMA((2, SUM_CUTS)),
        ],
        compiler_params=pltpu.CompilerParams(collective_id=1, has_side_effects=True, vmem_limit_bytes=LIMIT),
        name="sum_power",
    )(power.reshape(rows, PATCH)).reshape(2, PATCH, PATCH)


def back_kernel(total_ref, far_ref, windows_ref, modes_ref, measured_ref, offsets_ref, counts_ref, left_ref, right_ref,
                acc_ref, probe_ref):
    core = lax.axis_index("mode") % 2
    acc_ref[...] = jnp.zeros_like(acc_ref)
    for local in range(2):
        slot = 2 * core + local
        amplitude = jnp.sqrt(measured_ref[slot].astype(F32))
        live = (slot < counts_ref[0]).astype(F32)
        scaling = live * (1.0 - amplitude / jnp.sqrt(jnp.maximum(total_ref[local], 1.0)))
        win_real, win_imag = windows_ref[local, 0], windows_ref[local, 1]
        term_real = term_imag = None
        for pair in range(PAIR):
            back_real, back_imag = transform(
                scaling * far_ref[local, pair, 0], scaling * far_ref[local, pair, 1], left_ref, right_ref
            )
            mode_real, mode_imag = modes_ref[pair, 0], modes_ref[pair, 1]
            grad_real = mode_real * back_real + mode_imag * back_imag
            grad_imag = mode_real * back_imag - mode_imag * back_real
            term_real = grad_real if term_real is None else term_real + grad_real
            term_imag = grad_imag if term_imag is None else term_imag + grad_imag
            probe_real = win_real * back_real + win_imag * back_imag
            probe_imag = win_real * back_imag - win_imag * back_real
            if local == 0:
                probe_ref[pair, 0] = probe_real
                probe_ref[pair, 1] = probe_imag
            else:
                probe_ref[pair, 0] += probe_real
                probe_ref[pair, 1] += probe_imag
        rows, columns, down, right = corner(offsets_ref, slot)
        for part, term in enumerate((term_real, term_imag)):
            term = jnp.concatenate([term, jnp.zeros((TALL - PATCH, PATCH), F32)], axis=0)
            term = jnp.concatenate([pltpu.roll(term, down, 0), jnp.zeros((TALL, BROAD - PATCH), F32)], axis=1)
            acc_ref[part, rows, columns] += pltpu.roll(term, right, 1)


def back(total, far, windows, modes, measured, offsets, counts, left, right):
    return pl.pallas_call(
        back_kernel,
        out_shape=(
            jax.ShapeDtypeStruct((2, 2 * STRIP, WIDTH), F32),
            jax.ShapeDtypeStruct((PAIR, 2, PATCH, PATCH), F32),
        ),
        in_specs=[VMEM, VMEM, VMEM, VMEM, VMEM, SMEM, SMEM, VMEM, VMEM],
        out_specs=(VMEM, VMEM),
        compiler_params=pltpu.CompilerParams(vmem_limit_bytes=LIMIT),
        name="back",
    )(total, far, windows, modes, measured, offsets, counts, left, right)


def gather_kernel(tiles, grid_x, grid_z, acc_ref, terms_ref, object_ref, probe_ref, pair_buf, chain_out, chain_in,
                  probe_buf, mine, x_in, z_in, pair_send, pair_recv, chain_send, chain_recv, probe_send, probe_recv, x_send, x_recv, z_send, z_recv, h_send, h_recv, zg_send, zg_recv, xg_send,
                  xg_recv):
    tile, mode, chip, core = place()
    sibling = (tile, mode + 1 - 2 * core)
    after = lax.rem(tile + 1, tiles)
    before = lax.rem(tile + tiles - 1, tiles)
    to_up = (jnp.where(chip < 3, tile, after), jnp.where(chip < 3, mode + 2, core))
    from_up = (jnp.where(chip > 0, tile, before), jnp.where(chip > 0, mode - 2, core + 6))
    to_down = (jnp.where(chip > 0, tile, after), jnp.where(chip > 0, mode - 2, core + 6))
    from_down = (jnp.where(chip < 3, tile, before), jnp.where(chip < 3, mode + 2, core))

    high, plane = tile % 2, tile // 2
    at_z, at_x = plane % grid_z, plane // grid_z

    def at(x, z, h):
        return ((x * grid_z + z) * 2 + h, mode)

    x_peers = [lax.rem(at_x + step, grid_x) for step in range(1, grid_x)]
    z_peers = [lax.rem(at_z + step, grid_z) for step in range(1, grid_z)]
    x_ids = [at(peer, at_z, high) for peer in x_peers]
    z_ids = [at(at_x, peer, high) for peer in z_peers]
    h_id = at(at_x, at_z, 1 - high)
    greet([to_up, from_up, to_down, from_down, sibling, h_id] + x_ids + z_ids)

    probe_pair = remote(terms_ref.at[1 - core], probe_buf, probe_send, probe_recv, sibling)
    probe_pair.start()

    def pair_copy(block):
        return remote(
            acc_ref.at[:, 2 * block + 1 - core], pair_buf.at[:, block], pair_send.at[block], pair_recv.at[block], sibling
        )

    pair_order = (5, 6, 4, 7, 3, 0, 2, 1)
    for block in pair_order:
        pair_copy(block).start()

    depth_x = 2 * PATCH // grid_x
    depth_z = depth_x // grid_z
    probe_pair.wait()
    mine[...] = probe_buf[...] + terms_ref[core]

    def x_copy(step):
        peer = x_peers[step]
        return remote(
            mine.at[pl.ds(peer * depth_x, depth_x)], x_in.at[step], x_send.at[step], x_recv.at[step], x_ids[step]
        )

    for step in range(grid_x - 1):
        x_copy(step).start()

    def chain_copy(way, item):
        return remote(
            chain_out.at[way, item], chain_in.at[way, item], chain_send.at[way, item], chain_recv.at[way, item],
            (to_up, to_down)[way],
        )

    own_x = pl.ds(at_x * depth_x, depth_x)
    own_z = pl.ds(at_x * depth_x + at_z * depth_z, depth_z)

    def z_copy(step):
        rows = pl.ds(at_x * depth_x + z_peers[step] * depth_z, depth_z)
        return remote(mine.at[rows], z_in.at[step], z_send.at[step], z_recv.at[step], z_ids[step])

    h_copy = remote(mine.at[own_z], z_in.at[grid_z - 1], h_send, h_recv, h_id)

    def z_back(step, owner):
        rows = pl.ds(at_x * depth_x + owner * depth_z, depth_z)
        return remote(probe_ref.at[rows], probe_ref.at[rows], zg_send.at[step], zg_recv.at[step], z_ids[step])

    def x_back(step, owner):
        rows = pl.ds(owner * depth_x, depth_x)
        return remote(probe_ref.at[rows], probe_ref.at[rows], xg_send.at[step], xg_recv.at[step], x_ids[step])

    def after_x():
        for step in range(grid_x - 1):
            x_copy(step).wait()
        total = mine[own_x]
        for step in range(grid_x - 1):
            total = total + x_in[step]
        mine[own_x] = total
        for step in range(grid_z - 1):
            z_copy(step).start()

    def after_z():
        for step in range(grid_z - 1):
            z_copy(step).wait()
        total = mine[own_z]
        for step in range(grid_z - 1):
            total = total + z_in[step]
        mine[own_z] = total
        h_copy.start()

    def after_h():
        h_copy.wait()
        probe_ref[own_z] = mine[own_z] + z_in[grid_z - 1]
        for step in range(grid_z - 1):
            z_back(step, at_z).start()

    def after_z_back():
        for step in range(grid_z - 1):
            z_back(step, at_z).wait_send()
            z_back(step, lax.rem(at_z + grid_z - step - 1, grid_z)).wait_recv()
        for step in range(grid_x - 1):
            x_back(step, at_x).start()

    for here in range(CHIPS):
        @pl.when(chip == here)
        def _():
            ready = set()

            def part(block, half):
                if block not in ready:
                    ready.add(block)
                    pair_copy(block).wait()
                return pair_buf[half, block] + acc_ref[half, 2 * block + core]

            events = [(8.0, 2, after_x), (13.0, 3, after_z), (16.0, 4, after_h), (20.0, 5, after_z_back)]
            sums = {}

            def arrive(way, rank, item):
                chain_copy(way, item).wait_recv()
                block, half = chain_blocks(way)[item // 2], item % 2
                if rank == CHIPS - 1 and item >= 4 or item >= 4 and stays(item) == rank or rank == 0 and item // 2 == 1:
                    sums.setdefault(half, []).append(chain_in[way, item])
                elif rank == 0:
                    own = part(chain_blocks(way)[4], half)
                    send(way, 8 + half, own + chain_in[way, item])
                else:
                    send(way, item, part(block, half) + chain_in[way, item])

            def send(way, item, value):
                chain_out[way, item] = value
                chain_copy(way, item).start()

            for way, rank in ((0, here), (1, CHIPS - 1 - here)):
                for item, time in timetable(rank).items():
                    events.append((time, way, functools.partial(arrive, way, rank, item)))
            for item in range(8):
                for way, rank in ((0, here), (1, CHIPS - 1 - here)):
                    if rank == 0:
                        send(way, item, part(chain_blocks(way)[item // 2], item % 2))
            for _, _, action in sorted(events, key=lambda event: event[:2]):
                action()
            for half in range(2):
                result = part(here, half)
                for term in sums[half]:
                    result = result + term
                object_ref[half] = result
            for way, rank in ((0, here), (1, CHIPS - 1 - here)):
                for item in range(10):
                    if item < 4 or rank < stays(item):
                        chain_copy(way, item).wait_send()

    for step in range(grid_x - 1):
        x_back(step, at_x).wait_send()
        x_back(step, lax.rem(at_x + grid_x - step - 1, grid_x)).wait_recv()


def chain_blocks(way):
    return ((5, 4, 3, 2, 1), (6, 7, 0, 1, 2))[way]


def stays(item):
    return 5 - item // 2


def timetable(rank, step=2.05):
    spill = {}
    for _ in range(2):
        ready = [{item: 0.0 for item in range(8)}]
        if spill:
            ready[0].update({8 + half: spill[half] for half in range(2)})
        for at in range(CHIPS):
            clock, arrivals = 0.0, {}
            for item in range(10):
                if item in ready[at] and (item < 4 or at < stays(item)):
                    clock = max(clock, ready[at][item]) + step
                    arrivals[item] = clock + LATENCY
            ready.append(arrivals)
        spill = ready[CHIPS]
    return spill if rank == 0 else ready[rank]


def gather(tiles, grid_x, grid_z, acc, terms):
    rows = 2 * PATCH
    depth_x = rows // grid_x
    depth_z = depth_x // grid_z
    block = (2, 32, WIDTH)
    dma = pltpu.SemaphoreType.DMA
    object_rows, probe = pl.pallas_call(
        functools.partial(gather_kernel, tiles, grid_x, grid_z),
        out_shape=(jax.ShapeDtypeStruct(block, F32), jax.ShapeDtypeStruct((rows, PATCH), F32)),
        in_specs=[VMEM, VMEM],
        out_specs=(VMEM, VMEM),
        scratch_shapes=[
            pltpu.VMEM((2, 8, 32, WIDTH), F32),
            pltpu.VMEM((2, 10, 32, WIDTH), F32),
            pltpu.VMEM((2, 10, 32, WIDTH), F32),
            pltpu.VMEM((rows, PATCH), F32),
            pltpu.VMEM((rows, PATCH), F32),
            pltpu.VMEM((max(grid_x - 1, 1), depth_x, PATCH), F32),
            pltpu.VMEM((grid_z, depth_z, PATCH), F32),
            dma((8,)), dma((8,)),
            dma((2, 10)), dma((2, 10)),
            dma, dma,
            dma((max(grid_x - 1, 1),)), dma((max(grid_x - 1, 1),)),
            dma((grid_z,)), dma((grid_z,)),
            dma, dma,
            dma((grid_z,)), dma((grid_z,)),
            dma((max(grid_x - 1, 1),)), dma((max(grid_x - 1, 1),)),
        ],
        compiler_params=pltpu.CompilerParams(collective_id=2, has_side_effects=True, vmem_limit_bytes=LIMIT),
        name="gather",
    )(acc.reshape(2, 16, 32, WIDTH), terms.reshape(PAIR, rows, PATCH))
    return object_rows, probe.reshape(1, 2, PATCH, PATCH)


def solution(mesh):
    tiles = mesh.shape["tile"]
    grid_x = 4 if tiles == 64 else 2
    grid_z = tiles // 2 // grid_x
    left_forward, right_forward, left_back, right_back = dft_tables()

    def body(object_field, probe_modes, measured, offsets, counts):
        ext, modes = halo(tiles, object_field, probe_modes)
        windows, far, power = forward(ext, modes, offsets, jnp.asarray(left_forward), jnp.asarray(right_forward))
        total = sum_power(power)
        acc, terms = back(
            total, far, windows, modes, measured, offsets, counts, jnp.asarray(left_back), jnp.asarray(right_back)
        )
        return gather(tiles, grid_x, grid_z, acc, terms)

    return jax.shard_map(
        body,
        mesh=mesh,
        in_specs=(
            P(None, "tile", None),
            P("mode", None, None, None),
            P("tile", None, None),
            P("tile", None),
            P("tile"),
        ),
        out_specs=(P(None, ("tile", "mode"), None), P("mode", None, None, None)),
        check_vma=False,
    )
```

```python
import functools
import math

import jax
import jax.numpy as jnp
import numpy as np
from jax import lax
from jax.experimental import pallas as pl
from jax.experimental.pallas import tpu as pltpu
from jax.sharding import PartitionSpec as P

MESH = pl.DeviceIdType.MESH
F32 = jnp.float32
BF16 = jnp.bfloat16
VMEM = pl.BlockSpec(memory_space=pltpu.VMEM)
SMEM = pl.BlockSpec(memory_space=pltpu.SMEM)
ANY = pl.BlockSpec(memory_space=pl.ANY)
LIMIT = 56 * 1024 * 1024
PATCH = 256
STRIP = 256
WIDTH = 768
CAP = 4
CHIPS = 4
PAIR = 2

HALO_CUTS = 8
SUM_CUTS = 8
LATENCY = 2.3


def split(value):
    high = value.astype(BF16)
    return high, (value - high.astype(F32)).astype(BF16)


def dft_tables():
    index = np.arange(PATCH)
    angle = 2.0 * math.pi * ((index[:, None] * index[None, :]) % PATCH) / PATCH
    cos, sine = np.cos(angle) / math.sqrt(PATCH), -np.sin(angle) / math.sqrt(PATCH)

    def parts(block):
        high = block.astype(jnp.bfloat16)
        low = (block - high.astype(np.float64)).astype(jnp.bfloat16)
        return high, low

    high, low = parts(np.block([[cos, -sine], [sine, cos]]))
    left = np.concatenate([high, high, low], axis=1)
    high, low = parts(np.block([[cos, sine], [-sine, cos]]))
    right = np.concatenate([high, high, low], axis=0)
    return left, right


def transform(real, imag, left, right):
    high, low = split(jnp.concatenate([real, imag], axis=0))
    mid = jnp.dot(left[...], jnp.concatenate([high, low, high], axis=0), preferred_element_type=F32)
    high, low = split(jnp.concatenate([mid[:PATCH], mid[PATCH:]], axis=1))
    out = jnp.dot(jnp.concatenate([high, low, high], axis=1), right[...], preferred_element_type=F32)
    return out[:, :PATCH], out[:, PATCH:]


def selector(shape, source, target, offset):
    index = lax.broadcasted_iota(jnp.int32, shape, source) - lax.broadcasted_iota(jnp.int32, shape, target)
    return jnp.where(index == offset, 1.0, 0.0).astype(BF16)


def select(left, right):
    return jnp.dot(left, right, preferred_element_type=F32)


def remote(source, target, send_sem, recv_sem, device):
    return pltpu.make_async_remote_copy(
        src_ref=source, dst_ref=target, send_sem=send_sem, recv_sem=recv_sem, device_id=device, device_id_type=MESH
    )


def by_chip(chip, action):
    for here in range(CHIPS):
        pl.when(chip == here)(functools.partial(action, here))


def ranks(here):
    return ((0, here), (1, CHIPS - 1 - here))


def kernel(tiles, grid_x, grid_z, object_hbm, probe_hbm, measured_ref, offsets_ref, counts_ref, left_hbm, right_hbm,
           object_ref, probe_ref,
           ext, modes, left, right, windows, far, power, staged, arrived, cut_columns,
           cut_rows, put_columns, put_rows, strips, moved, acc, terms, pair_buf, chain_out,
           chain_in, probe_buf, mine, x_in, z_in, local_sem, swap_send, swap_recv, halo_send, halo_recv, cross_send,
           cross_recv, sum_send, sum_recv, pair_send, pair_recv, chain_send, chain_recv, probe_send, probe_recv, x_send,
           x_recv, z_send, z_recv, h_send, h_recv, zg_send, zg_recv, xg_send, xg_recv):
    tile, mode = lax.axis_index("tile"), lax.axis_index("mode")
    chip, core = mode // 2, mode % 2
    high, plane = tile % 2, tile // 2
    at_z, at_x = plane % grid_z, plane // grid_z
    after, before = lax.rem(tile + 1, tiles), lax.rem(tile + tiles - 1, tiles)
    sibling = (tile, mode + 1 - 2 * core)
    above = jnp.where(chip < 3, mode + 2, core)
    below = jnp.where(chip > 0, mode - 2, core + 6)
    next_above, last_above = (jnp.where(chip < 3, tile, after), above), (jnp.where(chip < 3, tile, before), above)
    next_below, last_below = (jnp.where(chip > 0, tile, after), below), (jnp.where(chip > 0, tile, before), below)

    def at(x, z, h):
        return ((x * grid_z + z) * 2 + h, mode)

    x_peers = [lax.rem(at_x + step, grid_x) for step in range(1, grid_x)]
    z_peers = [lax.rem(at_z + step, grid_z) for step in range(1, grid_z)]
    x_ids = [at(peer, at_z, high) for peer in x_peers]
    z_ids = [at(at_x, peer, high) for peer in z_peers]
    h_id = at(at_x, at_z, 1 - high)

    own_copy = pltpu.make_async_copy(object_hbm, ext.at[:, pl.ds(0, STRIP)], local_sem.at[0])
    probe_copy = pltpu.make_async_copy(probe_hbm.at[0], modes.at[core], local_sem.at[1])
    left_copy = pltpu.make_async_copy(left_hbm, left, local_sem.at[2])
    right_copy = pltpu.make_async_copy(right_hbm, right, local_sem.at[3])
    for copy in (own_copy, probe_copy, left_copy, right_copy):
        copy.start()
    barrier = pltpu.get_barrier_semaphore()
    friends = [next_above, last_above, next_below, last_below, sibling, h_id] + x_ids + z_ids
    for device in friends:
        pl.semaphore_signal(barrier, inc=1, device_id=device, device_id_type=MESH)
    pl.semaphore_wait(barrier, len(friends))

    swap = remote(probe_hbm.at[0], modes.at[core], swap_send, swap_recv, sibling)
    depth = STRIP // 4 // HALO_CUTS
    down_first = (last_below, last_above)

    def halo_rows(way, cut, owner):
        return (2 * way + owner) * (STRIP // 4) + cut * depth

    def halo_copy(way, cut, base):
        row = halo_rows(way, cut, core)
        return remote(
            ext.at[:, pl.ds(base + row, depth)],
            ext.at[:, pl.ds(STRIP + row, depth)],
            halo_send.at[way, cut],
            halo_recv.at[way, cut],
            down_first[way],
        )

    def cross_copy(way, cut, owner):
        block = ext.at[:, pl.ds(STRIP + halo_rows(way, cut, owner), depth)]
        return remote(block, block, cross_send.at[way, cut], cross_recv.at[way, cut], sibling)

    own_copy.wait()
    for way, last in ((0, 0), (1, 3)):
        @pl.when(chip == last)
        def _():
            for cut in range(HALO_CUTS):
                halo_copy(way, cut, 0).start()
    swap.start()
    for slot in range(2):
        row, column = offsets_ref[2 * core + slot, 0], offsets_ref[2 * core + slot, 1]
        own = pl.ds(slot * PATCH, PATCH)
        cut_columns[:, own] = selector((WIDTH, PATCH), 0, 1, column)
        put_columns[slot] = selector((PATCH, WIDTH), 1, 0, column)
        for copy in range(2):
            cut_rows[slot, :, pl.ds(copy * 2 * STRIP, 2 * STRIP)] = selector((PATCH, 2 * STRIP), 1, 0, row)
            put_rows[:, pl.ds((2 * copy + slot) * PATCH, PATCH)] = selector((2 * STRIP, PATCH), 0, 1, row)

    def cut_strip(first):
        for part in range(2):
            for index, value in enumerate(split(ext[part, pl.ds(first, STRIP)])):
                strips[part, pl.ds(index * 2 * STRIP + first, STRIP)] = select(value, cut_columns[...]).astype(BF16)

    cut_strip(0)

    def halo_events(here):
        step = 8.0 / HALO_CUTS
        events = []
        for way, rank in ((0, CHIPS - 1 - here), (1, here)):
            for cut in range(HALO_CUTS):
                events.append(((rank + 1) * (step + LATENCY) + cut * step, way, cut, rank < CHIPS - 1))
        for _, way, cut, forwards in sorted(events):
            halo_copy(way, cut, 0).wait_recv()
            if forwards:
                halo_copy(way, cut, STRIP).start()
            cross_copy(way, cut, core).start()

    by_chip(chip, halo_events)
    probe_copy.wait()
    swap.wait_recv()
    left_copy.wait()
    right_copy.wait()
    for cut in range(HALO_CUTS):
        for way in range(2):
            cross_copy(way, cut, 1 - core).wait_recv()

    sum_depth = PATCH // SUM_CUTS

    def sum_copy(way, slot, cut, source):
        rows = pl.ds(cut * sum_depth, sum_depth)
        item = slot * SUM_CUTS + cut
        return remote(
            source.at[slot, rows],
            arrived.at[way, slot, rows],
            sum_send.at[way, item],
            sum_recv.at[way, item],
            ((tile, mode + 2), (tile, mode - 2))[way],
        )

    def forward(slot):
        window = []
        for part in range(2):
            block = select(cut_rows[slot], strips[part, :, pl.ds(slot * PATCH, PATCH)])
            windows[slot, part] = block
            window.append(block)
        for pair in range(PAIR):
            mode_real, mode_imag = modes[pair, 0], modes[pair, 1]
            far_real, far_imag = transform(
                mode_real * window[0] - mode_imag * window[1],
                mode_real * window[1] + mode_imag * window[0],
                left,
                right,
            )
            far[slot, pair, 0] = far_real
            far[slot, pair, 1] = far_imag
            if pair == 0:
                power[slot] = far_real * far_real + far_imag * far_imag
            else:
                power[slot] += far_real * far_real + far_imag * far_imag

    def first_sums(slot):
        for way, first in ((0, 0), (1, 3)):
            @pl.when(chip == first)
            def _():
                for cut in range(SUM_CUTS):
                    sum_copy(way, slot, cut, power).start()

    cut_strip(STRIP)
    for slot in range(2):
        forward(slot)
        first_sums(slot)

    def sum_events(here):
        step = 5.3 / SUM_CUTS
        events = []
        for way, rank in ranks(here):
            if rank > 0:
                for slot in range(2):
                    for cut in range(SUM_CUTS):
                        time = rank * (step + LATENCY) + (slot * SUM_CUTS + cut) * step
                        events.append((time, way, slot, cut, rank < CHIPS - 1))
        for _, way, slot, cut, forwards in sorted(events):
            sum_copy(way, slot, cut, power).wait_recv()
            if forwards:
                rows = pl.ds(cut * sum_depth, sum_depth)
                staged[way, slot, rows] = power[slot, rows] + arrived[way, slot, rows]
                sum_copy(way, slot, cut, staged.at[way]).start()

    by_chip(chip, sum_events)

    def intensity(slot):
        lower = jnp.where(chip > 0, arrived[0, slot], 0.0)
        upper = jnp.where(chip < 3, arrived[1, slot], 0.0)
        return power[slot] + (lower + upper)

    def backward(slot):
        index = 2 * core + slot
        amplitude = jnp.sqrt(measured_ref[index].astype(F32))
        live = (index < counts_ref[0]).astype(F32)
        scaling = live * (1.0 - amplitude / jnp.sqrt(jnp.maximum(intensity(slot), 1.0)))
        win_real, win_imag = windows[slot, 0], windows[slot, 1]
        sums = None
        for pair in range(PAIR):
            back_real, minus_imag = transform(
                scaling * far[slot, pair, 0], -(scaling * far[slot, pair, 1]), left, right
            )
            mode_real, mode_imag = modes[pair, 0], modes[pair, 1]
            grads = (
                mode_real * back_real - mode_imag * minus_imag,
                -(mode_real * minus_imag + mode_imag * back_real),
            )
            sums = grads if sums is None else (sums[0] + grads[0], sums[1] + grads[1])
            probe_real = win_real * back_real - win_imag * minus_imag
            probe_imag = -(win_real * minus_imag + win_imag * back_real)
            if slot == 0:
                terms[pair, pl.ds(0, PATCH)] = probe_real
                terms[pair, pl.ds(PATCH, PATCH)] = probe_imag
            else:
                terms[pair, pl.ds(0, PATCH)] += probe_real
                terms[pair, pl.ds(PATCH, PATCH)] += probe_imag
        for part, term in enumerate(sums):
            for copy, value in enumerate(split(term)):
                rows = pl.ds((2 * copy + slot) * PATCH, PATCH)
                moved[part, rows] = select(value, put_columns[slot]).astype(BF16)

    for slot in range(2):
        backward(slot)

    probe_pair = remote(terms.at[1 - core], probe_buf, probe_send, probe_recv, sibling)
    probe_pair.start()

    def pair_copy(block):
        return remote(
            acc.at[:, 2 * block + 1 - core], pair_buf.at[:, block], pair_send.at[block], pair_recv.at[block], sibling
        )

    for first, blocks in ((STRIP, (5, 6, 4, 7)), (0, (3, 0, 2, 1))):
        for half in range(2):
            total = select(put_rows[pl.ds(first, STRIP)], moved[half])
            for index in range(8):
                acc[half, first // 32 + index] = total[32 * index : 32 * index + 32]
        for block in blocks:
            pair_copy(block).start()

    depth_x = 2 * PATCH // grid_x
    depth_z = depth_x // grid_z
    probe_pair.wait_recv()
    mine[...] = probe_buf[...] + terms[core]

    def x_copy(step):
        peer = x_peers[step]
        return remote(
            mine.at[pl.ds(peer * depth_x, depth_x)], x_in.at[step], x_send.at[step], x_recv.at[step], x_ids[step]
        )

    for step in range(grid_x - 1):
        x_copy(step).start()

    def chain_copy(way, item):
        return remote(
            chain_out.at[way, item], chain_in.at[way, item], chain_send.at[way, item], chain_recv.at[way, item],
            (next_above, next_below)[way],
        )

    own_x = pl.ds(at_x * depth_x, depth_x)
    own_z = pl.ds(at_x * depth_x + at_z * depth_z, depth_z)

    def z_copy(step):
        rows = pl.ds(at_x * depth_x + z_peers[step] * depth_z, depth_z)
        return remote(mine.at[rows], z_in.at[step], z_send.at[step], z_recv.at[step], z_ids[step])

    h_copy = remote(mine.at[own_z], z_in.at[grid_z - 1], h_send, h_recv, h_id)

    def z_back(step, owner):
        rows = pl.ds(at_x * depth_x + owner * depth_z, depth_z)
        return remote(probe_ref.at[rows], probe_ref.at[rows], zg_send.at[step], zg_recv.at[step], z_ids[step])

    def x_back(step, owner):
        rows = pl.ds(owner * depth_x, depth_x)
        return remote(probe_ref.at[rows], probe_ref.at[rows], xg_send.at[step], xg_recv.at[step], x_ids[step])

    def after_x():
        for step in range(grid_x - 1):
            x_copy(step).wait()
        total = mine[own_x]
        for step in range(grid_x - 1):
            total = total + x_in[step]
        mine[own_x] = total
        for step in range(grid_z - 1):
            z_copy(step).start()

    def after_z():
        for step in range(grid_z - 1):
            z_copy(step).wait()
        total = mine[own_z]
        for step in range(grid_z - 1):
            total = total + z_in[step]
        mine[own_z] = total
        h_copy.start()

    def after_h():
        h_copy.wait()
        probe_ref[own_z] = mine[own_z] + z_in[grid_z - 1]
        for step in range(grid_z - 1):
            z_back(step, at_z).start()

    def after_z_back():
        for step in range(grid_z - 1):
            z_back(step, at_z).wait_send()
            z_back(step, lax.rem(at_z + grid_z - step - 1, grid_z)).wait_recv()
        for step in range(grid_x - 1):
            x_back(step, at_x).start()

    def chain_events(here):
        ready = set()

        def part(block, half):
            if block not in ready:
                ready.add(block)
                pair_copy(block).wait_recv()
            return pair_buf[half, block] + acc[half, 2 * block + core]

        def send(way, item, value):
            chain_out[way, item] = value
            chain_copy(way, item).start()

        sums = {}

        def arrive(way, rank, item):
            chain_copy(way, item).wait_recv()
            blocks, half = chain_blocks(way), item % 2
            if item >= 4 and stays(item) == rank or rank == 0 and item // 2 == 1:
                sums.setdefault(half, []).append(chain_in[way, item])
            elif rank == 0:
                send(way, 8 + half, part(blocks[4], half) + chain_in[way, item])
            else:
                send(way, item, part(blocks[item // 2], half) + chain_in[way, item])

        for item in range(8):
            for way, rank in ranks(here):
                if rank == 0:
                    send(way, item, part(chain_blocks(way)[item // 2], item % 2))
        events = [(8.0, 2, after_x), (13.0, 3, after_z), (16.0, 4, after_h), (20.0, 5, after_z_back)]
        for way, rank in ranks(here):
            for item, time in timetable(rank).items():
                events.append((time, way, functools.partial(arrive, way, rank, item)))
        for _, _, action in sorted(events, key=lambda event: event[:2]):
            action()
        for half in range(2):
            result = part(here, half)
            for term in sums[half]:
                result = result + term
            object_ref[half] = result

    by_chip(chip, chain_events)
    for step in range(grid_x - 1):
        x_back(step, lax.rem(at_x + grid_x - step - 1, grid_x)).wait_recv()

    def sends(here):
        for way, rank in ranks(here):
            for item in range(10):
                if item < 4 or rank < stays(item):
                    chain_copy(way, item).wait_send()
            if rank < CHIPS - 1:
                for slot in range(2):
                    for cut in range(SUM_CUTS):
                        sum_copy(way, slot, cut, power).wait_send()

    by_chip(chip, sends)
    swap.wait_send()
    probe_pair.wait_send()
    for cut in range(HALO_CUTS):
        for way in range(2):
            halo_copy(way, cut, 0).wait_send()
            cross_copy(way, cut, core).wait_send()
    for block in range(8):
        pair_copy(block).wait_send()
    for step in range(grid_x - 1):
        x_back(step, at_x).wait_send()


def chain_blocks(way):
    return ((5, 4, 3, 2, 1), (6, 7, 0, 1, 2))[way]


def stays(item):
    return 5 - item // 2


def timetable(rank, step=2.05):
    spill = {}
    for _ in range(2):
        ready = [{item: 0.0 for item in range(8)}]
        if spill:
            ready[0].update({8 + half: spill[half] for half in range(2)})
        for at in range(CHIPS):
            clock, arrivals = 0.0, {}
            for item in range(10):
                if item in ready[at] and (item < 4 or at < stays(item)):
                    clock = max(clock, ready[at][item]) + step
                    arrivals[item] = clock + LATENCY
            ready.append(arrivals)
        spill = ready[CHIPS]
    return spill if rank == 0 else ready[rank]


def solution(mesh):
    tiles = mesh.shape["tile"]
    grid_x = 4 if tiles == 64 else 2
    grid_z = tiles // 2 // grid_x
    left, right = dft_tables()
    rows = 2 * PATCH
    depth_x = rows // grid_x
    depth_z = depth_x // grid_z
    block = (2, 32, WIDTH)
    dma = pltpu.SemaphoreType.DMA

    def body(object_field, probe_modes, measured, offsets, counts):
        object_rows, probe = pl.pallas_call(
            functools.partial(kernel, tiles, grid_x, grid_z),
            out_shape=(jax.ShapeDtypeStruct(block, F32), jax.ShapeDtypeStruct((rows, PATCH), F32)),
            in_specs=[ANY, ANY, VMEM, SMEM, SMEM, ANY, ANY],
            out_specs=(VMEM, VMEM),
            scratch_shapes=[
                pltpu.VMEM((2, 2 * STRIP, WIDTH), F32),
                pltpu.VMEM((PAIR, 2, PATCH, PATCH), F32),
                pltpu.VMEM(left.shape, BF16),
                pltpu.VMEM(right.shape, BF16),
                pltpu.VMEM((2, 2, PATCH, PATCH), F32),
                pltpu.VMEM((2, PAIR, 2, PATCH, PATCH), F32),
                pltpu.VMEM((2, PATCH, PATCH), F32),
                pltpu.VMEM((2, 2, PATCH, PATCH), F32),
                pltpu.VMEM((2, 2, PATCH, PATCH), F32),
                pltpu.VMEM((WIDTH, 2 * PATCH), BF16),
                pltpu.VMEM((2, PATCH, 4 * STRIP), BF16),
                pltpu.VMEM((2, PATCH, WIDTH), BF16),
                pltpu.VMEM((2 * STRIP, 4 * PATCH), BF16),
                pltpu.VMEM((2, 4 * STRIP, 2 * PATCH), BF16),
                pltpu.VMEM((2, 4 * PATCH, WIDTH), BF16),
                pltpu.VMEM((2, 16, 32, WIDTH), F32),
                pltpu.VMEM((PAIR, rows, PATCH), F32),
                pltpu.VMEM((2, 8, 32, WIDTH), F32),
                pltpu.VMEM((2, 10, 32, WIDTH), F32),
                pltpu.VMEM((2, 10, 32, WIDTH), F32),
                pltpu.VMEM((rows, PATCH), F32),
                pltpu.VMEM((rows, PATCH), F32),
                pltpu.VMEM((grid_x - 1, depth_x, PATCH), F32),
                pltpu.VMEM((grid_z, depth_z, PATCH), F32),
                dma((4,)),
                dma, dma,
                dma((2, HALO_CUTS)), dma((2, HALO_CUTS)),
                dma((2, HALO_CUTS)), dma((2, HALO_CUTS)),
                dma((2, 2 * SUM_CUTS)), dma((2, 2 * SUM_CUTS)),
                dma((8,)), dma((8,)),
                dma((2, 10)), dma((2, 10)),
                dma, dma,
                dma((grid_x - 1,)), dma((grid_x - 1,)),
                dma((grid_z,)), dma((grid_z,)),
                dma, dma,
                dma((grid_z,)), dma((grid_z,)),
                dma((grid_x - 1,)), dma((grid_x - 1,)),
            ],
            compiler_params=pltpu.CompilerParams(collective_id=0, has_side_effects=True, vmem_limit_bytes=LIMIT),
            name="ptychography",
        )(object_field, probe_modes, measured, offsets, counts, jnp.asarray(left), jnp.asarray(right))
        return object_rows, probe.reshape(1, 2, PATCH, PATCH)

    return jax.shard_map(
        body,
        mesh=mesh,
        in_specs=(
            P(None, "tile", None),
            P("mode", None, None, None),
            P("tile", None, None),
            P("tile", None),
            P("tile"),
        ),
        out_specs=(P(None, ("tile", "mode"), None), P("mode", None, None, None)),
        check_vma=False,
    )
```

```python
import functools
import math

import jax
import jax.numpy as jnp
import numpy as np
from jax import lax
from jax.experimental import pallas as pl
from jax.experimental.pallas import tpu as pltpu
from jax.sharding import PartitionSpec as P

MESH = pl.DeviceIdType.MESH
F32 = jnp.float32
BF16 = jnp.bfloat16
VMEM = pl.BlockSpec(memory_space=pltpu.VMEM)
SMEM = pl.BlockSpec(memory_space=pltpu.SMEM)
ANY = pl.BlockSpec(memory_space=pl.ANY)
LIMIT = 56 * 1024 * 1024
PATCH = 256
STRIP = 256
WIDTH = 768
CAP = 4
CHIPS = 4
PAIR = 2

HALO_CUTS = 8
SUM_CUTS = 8
LATENCY = 2.3


def split(value):
    high = value.astype(BF16)
    return high, (value - high.astype(F32)).astype(BF16)


def dft_tables():
    index = np.arange(PATCH)
    angle = 2.0 * math.pi * ((index[:, None] * index[None, :]) % PATCH) / PATCH
    cos, sine = np.cos(angle) / math.sqrt(PATCH), -np.sin(angle) / math.sqrt(PATCH)

    def parts(block):
        high = block.astype(jnp.bfloat16)
        low = (block - high.astype(np.float64)).astype(jnp.bfloat16)
        return high, low

    high, low = parts(np.block([[cos, -sine], [sine, cos]]))
    left = np.concatenate([high, high, low], axis=1)
    high, low = parts(np.block([[cos, sine], [-sine, cos]]))
    right = np.concatenate([high, high, low], axis=0)
    return left, right


def transform(real, imag, left, right):
    high, low = split(jnp.concatenate([real, imag], axis=0))
    mid = jnp.dot(left[...], jnp.concatenate([high, low, high], axis=0), preferred_element_type=F32)
    high, low = split(jnp.concatenate([mid[:PATCH], mid[PATCH:]], axis=1))
    out = jnp.dot(jnp.concatenate([high, low, high], axis=1), right[...], preferred_element_type=F32)
    return out[:, :PATCH], out[:, PATCH:]


def selector(shape, source, target, offset):
    index = lax.broadcasted_iota(jnp.int32, shape, source) - lax.broadcasted_iota(jnp.int32, shape, target)
    return jnp.where(index == offset, 1.0, 0.0).astype(BF16)


def select(left, right):
    return jnp.dot(left, right, preferred_element_type=F32)


def remote(source, target, send_sem, recv_sem, device):
    return pltpu.make_async_remote_copy(
        src_ref=source, dst_ref=target, send_sem=send_sem, recv_sem=recv_sem, device_id=device, device_id_type=MESH
    )


def by_chip(chip, action):
    for here in range(CHIPS):
        pl.when(chip == here)(functools.partial(action, here))


def ranks(here):
    return ((0, here), (1, CHIPS - 1 - here))


def kernel(tiles, grid_x, grid_z, object_hbm, probe_hbm, measured_ref, offsets_ref, counts_ref, left_hbm, right_hbm,
           object_ref, probe_ref,
           ext, modes, left, right, windows, far, power, staged, arrived, cut_columns,
           cut_rows, put_columns, put_rows, strips, moved, acc, terms, pair_buf, chain_out,
           chain_in, probe_buf, mine, result, px_in, qz_in, pz_in, qx_in, local_sem, swap_send, swap_recv, halo_send, halo_recv, cross_send,
           cross_recv, sum_send, sum_recv, pair_send, pair_recv, chain_send, chain_recv, probe_send, probe_recv, px_send,
           px_recv, qz_send, qz_recv, pz_send, pz_recv, qx_send, qx_recv):
    tile, mode = lax.axis_index("tile"), lax.axis_index("mode")
    chip, core = mode // 2, mode % 2
    high, plane = tile % 2, tile // 2
    at_z, at_x = plane % grid_z, plane // grid_z
    after, before = lax.rem(tile + 1, tiles), lax.rem(tile + tiles - 1, tiles)
    sibling = (tile, mode + 1 - 2 * core)
    above = jnp.where(chip < 3, mode + 2, core)
    below = jnp.where(chip > 0, mode - 2, core + 6)
    next_above, last_above = (jnp.where(chip < 3, tile, after), above), (jnp.where(chip < 3, tile, before), above)
    next_below, last_below = (jnp.where(chip > 0, tile, after), below), (jnp.where(chip > 0, tile, before), below)

    def at(x, z, h):
        return ((x * grid_z + z) * 2 + h, mode)

    own_copy = pltpu.make_async_copy(object_hbm, ext.at[:, pl.ds(0, STRIP)], local_sem.at[0])
    probe_copy = pltpu.make_async_copy(probe_hbm.at[0], modes.at[core], local_sem.at[1])
    left_copy = pltpu.make_async_copy(left_hbm, left, local_sem.at[2])
    right_copy = pltpu.make_async_copy(right_hbm, right, local_sem.at[3])
    for copy in (own_copy, probe_copy, left_copy, right_copy):
        copy.start()
    barrier = pltpu.get_barrier_semaphore()
    friends = [next_above, last_above, next_below, last_below, sibling]
    friends += [at(lax.rem(at_x + step, grid_x), at_z, high) for step in range(1, grid_x)]
    friends += [at(lax.rem(at_x + step, grid_x), at_z, 1 - high) for step in range(grid_x)]
    friends += [at(at_x, lax.rem(at_z + step, grid_z), high) for step in range(1, grid_z)]
    friends += [at(at_x, lax.rem(at_z + step, grid_z), 1 - high) for step in range(1, grid_z)]
    for device in friends:
        pl.semaphore_signal(barrier, inc=1, device_id=device, device_id_type=MESH)
    pl.semaphore_wait(barrier, len(friends))

    swap = remote(probe_hbm.at[0], modes.at[core], swap_send, swap_recv, sibling)
    depth = STRIP // 4 // HALO_CUTS
    down_first = (last_below, last_above)

    def halo_rows(way, cut, owner):
        return (2 * way + owner) * (STRIP // 4) + cut * depth

    def halo_copy(way, cut, base):
        row = halo_rows(way, cut, core)
        return remote(
            ext.at[:, pl.ds(base + row, depth)],
            ext.at[:, pl.ds(STRIP + row, depth)],
            halo_send.at[way, cut],
            halo_recv.at[way, cut],
            down_first[way],
        )

    def cross_copy(way, cut, owner):
        block = ext.at[:, pl.ds(STRIP + halo_rows(way, cut, owner), depth)]
        return remote(block, block, cross_send, cross_recv, sibling)

    own_copy.wait()
    for way, last in ((0, 0), (1, 3)):
        @pl.when(chip == last)
        def _():
            for cut in range(HALO_CUTS):
                halo_copy(way, cut, 0).start()
    swap.start()
    for slot in range(2):
        row, column = offsets_ref[0, 2 * core + slot], offsets_ref[1, 2 * core + slot]
        own = pl.ds(slot * PATCH, PATCH)
        cut_columns[:, own] = selector((WIDTH, PATCH), 0, 1, column)
        put_columns[slot] = selector((PATCH, WIDTH), 1, 0, column)
        for copy in range(2):
            cut_rows[slot, :, pl.ds(copy * 2 * STRIP, 2 * STRIP)] = selector((PATCH, 2 * STRIP), 1, 0, row)
            put_rows[:, pl.ds((2 * copy + slot) * PATCH, PATCH)] = selector((2 * STRIP, PATCH), 0, 1, row)

    def cut_strip(part, first, depth):
        for index, value in enumerate(split(ext[part, pl.ds(first, depth)])):
            strips[part, pl.ds(index * 2 * STRIP + first, depth)] = select(value, cut_columns[...]).astype(BF16)

    def halo_events(here):
        step = 8.0 / HALO_CUTS
        events = []
        for way, rank in ((0, CHIPS - 1 - here), (1, here)):
            for cut in range(HALO_CUTS):
                events.append(((rank + 1) * (step + LATENCY) + cut * step, way, cut, rank < CHIPS - 1))
        for index, (_, way, cut, forwards) in enumerate(sorted(events)):
            halo_copy(way, cut, 0).wait_recv()
            if forwards:
                halo_copy(way, cut, STRIP).start()
            cross_copy(way, cut, core).start()
            if index in (1, 4, 7, 10):
                piece = (1, 4, 7, 10).index(index)
                cut_strip(piece // 2, piece % 2 * 128, 128)

    by_chip(chip, halo_events)
    probe_copy.wait()
    swap.wait_recv()
    left_copy.wait()
    right_copy.wait()
    crossed = ext.at[:, pl.ds(STRIP, STRIP // 2)]
    all_across = remote(crossed, crossed, cross_send, cross_recv, sibling)
    all_across.wait_recv()

    sum_depth = PATCH // SUM_CUTS

    def sum_copy(way, slot, cut, source):
        rows = pl.ds(cut * sum_depth, sum_depth)
        item = slot * SUM_CUTS + cut
        return remote(
            source.at[slot, rows],
            arrived.at[way, slot, rows],
            sum_send.at[way, item],
            sum_recv.at[way, item],
            ((tile, mode + 2), (tile, mode - 2))[way],
        )

    def forward(slot):
        window = []
        for part in range(2):
            block = select(cut_rows[slot], strips[part, :, pl.ds(slot * PATCH, PATCH)])
            windows[slot, part] = block
            window.append(block)
        for pair in range(PAIR):
            mode_real, mode_imag = modes[pair, 0], modes[pair, 1]
            far_real, far_imag = transform(
                mode_real * window[0] - mode_imag * window[1],
                mode_real * window[1] + mode_imag * window[0],
                left,
                right,
            )
            far[slot, pair, 0] = far_real
            far[slot, pair, 1] = far_imag
            if pair == 0:
                power[slot] = far_real * far_real + far_imag * far_imag
            else:
                power[slot] += far_real * far_real + far_imag * far_imag

    def first_sums(slot):
        for way, first in ((0, 0), (1, 3)):
            @pl.when(chip == first)
            def _():
                for cut in range(SUM_CUTS):
                    sum_copy(way, slot, cut, power).start()

    for part in range(2):
        cut_strip(part, STRIP, STRIP)
    for slot in range(2):
        forward(slot)
        first_sums(slot)

    def sum_events(late, here):
        step = 5.3 / SUM_CUTS
        events = []
        for way, rank in ranks(here):
            if rank > 0:
                for slot in range(2):
                    for cut in range(SUM_CUTS):
                        time = rank * (step + LATENCY) + (slot * SUM_CUTS + cut) * step
                        events.append((time, way, slot, cut, rank < CHIPS - 1))
        for _, way, slot, cut, forwards in sorted(events):
            if late != (not forwards and slot == 1):
                continue
            sum_copy(way, slot, cut, power).wait_recv()
            if forwards:
                rows = pl.ds(cut * sum_depth, sum_depth)
                staged[way, slot, rows] = power[slot, rows] + arrived[way, slot, rows]
                sum_copy(way, slot, cut, staged.at[way]).start()

    def intensity(slot):
        lower = jnp.where(chip > 0, arrived[0, slot], 0.0)
        upper = jnp.where(chip < 3, arrived[1, slot], 0.0)
        return power[slot] + (lower + upper)

    def backward(slot):
        index = 2 * core + slot
        amplitude = jnp.sqrt(measured_ref[index].astype(F32))
        live = (index < counts_ref[0]).astype(F32)
        scaling = live * (1.0 - amplitude / jnp.sqrt(jnp.maximum(intensity(slot), 1.0)))
        win_real, win_imag = windows[slot, 0], windows[slot, 1]
        sums = None
        for pair in (1 - core, core):
            back_real, minus_imag = transform(
                scaling * far[slot, pair, 0], -(scaling * far[slot, pair, 1]), left, right
            )
            mode_real, mode_imag = modes[pair, 0], modes[pair, 1]
            grads = (
                mode_real * back_real - mode_imag * minus_imag,
                -(mode_real * minus_imag + mode_imag * back_real),
            )
            sums = grads if sums is None else (sums[0] + grads[0], sums[1] + grads[1])
            probe_real = win_real * back_real - win_imag * minus_imag
            probe_imag = -(win_real * minus_imag + win_imag * back_real)
            if slot == 0:
                terms[pair, pl.ds(0, PATCH)] = probe_real
                terms[pair, pl.ds(PATCH, PATCH)] = probe_imag
            else:
                terms[pair, pl.ds(0, PATCH)] += probe_real
                terms[pair, pl.ds(PATCH, PATCH)] += probe_imag
                if pair is not core:
                    probe_pair.start()
        for part, term in enumerate(sums):
            for copy, value in enumerate(split(term)):
                rows = pl.ds((2 * copy + slot) * PATCH, PATCH)
                moved[part, rows] = select(value, put_columns[slot]).astype(BF16)

    probe_pair = remote(terms.at[1 - core], probe_buf, probe_send, probe_recv, sibling)
    swap.wait_send()
    all_across.wait_send()
    for cut in range(HALO_CUTS):
        for way in range(2):
            halo_copy(way, cut, 0).wait_send()
    by_chip(chip, functools.partial(sum_events, False))
    backward(0)
    by_chip(chip, functools.partial(sum_events, True))
    backward(1)

    def pair_copy(block):
        return remote(
            acc.at[:, 2 * block + 1 - core], pair_buf.at[:, block], pair_send.at[block], pair_recv.at[block], sibling
        )

    def put(first, blocks):
        for half in range(2):
            total = select(put_rows[pl.ds(first, STRIP)], moved[half])
            for index in range(8):
                acc[half, first // 32 + index] = total[32 * index : 32 * index + 32]
        for block in blocks:
            pair_copy(block).start()

    def group_x(index):
        return at(index, at_z, high)

    def group_z(index):
        return at(at_x, index, high)

    def group_zh(index):
        return at(at_x, index // 2, index % 2)

    def group_xh(index):
        return at(index // 2, at_z, index % 2)

    half_tiles = mine.shape[0] // 2
    x_tiles, z_tiles = half_tiles // grid_x, half_tiles // grid_z
    outer = (
        (group_x, grid_x, at_x, 0, x_tiles, px_in, px_send, px_recv),
        (group_z, grid_z, at_z, half_tiles, z_tiles, qz_in, qz_send, qz_recv),
    )
    inner = (
        (group_zh, 2 * grid_z, 2 * at_z + high, at_x * x_tiles, x_tiles // (2 * grid_z), pz_in, pz_send, pz_recv),
        (group_xh, 2 * grid_x, 2 * at_x + high, half_tiles + at_z * z_tiles, z_tiles // (2 * grid_x), qx_in, qx_send,
         qx_recv),
    )

    def scatter_copy(stage, step):
        group, count, here, base, depth, inbox, send, recv = stage
        peer = lax.rem(here + step + 1, count)
        return remote(mine.at[pl.ds(base + peer * depth, depth)], inbox.at[step], send.at[0], recv.at[0], group(peer))

    def back_copy(stage, step):
        group, count, here, base, depth, inbox, send, recv = stage
        rows = result.at[pl.ds(base + here * depth, depth)]
        return remote(rows, rows, send.at[1], recv.at[1], group(lax.rem(here + step + 1, count)))

    def all_of(stage, turn):
        group, count, here, base, depth, inbox, send, recv = stage
        if turn == 0:
            block = inbox.at[pl.ds(0, count - 1)]
        else:
            block = result.at[pl.ds(0, (count - 1) * depth)]
        return remote(block, block, send.at[turn], recv.at[turn], sibling)

    def steps(stages):
        order = [(min(step + 1, stage[1] - step - 1), step, stage) for stage in stages for step in range(stage[1] - 1)]
        return [(stage, step) for _, step, stage in sorted(order, key=lambda entry: entry[:2])]

    def scatter(stages):
        for stage, step in steps(stages):
            scatter_copy(stage, step).start()

    def collect(stages, target):
        for stage in stages:
            if stage[1] > 1:
                all_of(stage, 0).wait_recv()
            group, count, here, base, depth, inbox, send, recv = stage
            rows = pl.ds(base + here * depth, depth)
            total = mine[rows]
            for step in range(count - 1):
                total = total + inbox[step]
            target[rows] = total

    def spread(stages):
        for stage, step in steps(stages):
            back_copy(stage, step).start()

    def settle(stages):
        for stage in stages:
            if stage[1] > 1:
                all_of(stage, 1).wait_recv()

    def after_outer():
        collect(outer, mine)
        scatter(inner)

    def after_inner():
        collect(inner, result)
        spread(inner)

    def after_spread():
        settle(inner)
        spread(outer)

    probe_pair.wait_recv()
    for part in range(2):
        rows = pl.ds(part * PATCH, PATCH)
        total = probe_buf[rows] + terms[core, rows]
        for side in range(2):
            tiles_of = total[:, side * 128 : side * 128 + 128].reshape(PATCH // 8, 8, 128)
            mine[pl.ds(part * half_tiles + side * PATCH // 8, PATCH // 8)] = tiles_of
    scatter(outer)
    put(STRIP, (5, 6, 4, 7))

    def chain_copy(way, item):
        return remote(
            chain_out.at[way, item], chain_in.at[way, item], chain_send.at[way, item], chain_recv.at[way, item],
            (next_above, next_below)[way],
        )

    def first_rows(here):
        for item in range(4):
            for way, rank in ranks(here):
                if rank == 0:
                    block, half = chain_blocks(way)[item // 2], item % 2
                    if half == 0:
                        pair_copy(block).wait_recv()
                    chain_out[way, item] = pair_buf[half, block] + acc[half, 2 * block + core]
                    chain_copy(way, item).start()

    by_chip(chip, first_rows)
    put(0, (3, 0, 2, 1))

    def chain_events(here):
        ready = {block for way, rank in ranks(here) if rank == 0 for block in chain_blocks(way)[:2]}

        def part(block, half):
            if block not in ready:
                ready.add(block)
                pair_copy(block).wait_recv()
            return pair_buf[half, block] + acc[half, 2 * block + core]

        def send(way, item, value):
            chain_out[way, item] = value
            chain_copy(way, item).start()

        sums = {}

        def arrive(way, rank, item):
            chain_copy(way, item).wait_recv()
            blocks, half = chain_blocks(way), item % 2
            if item >= 4 and stays(item) == rank or rank == 0 and item // 2 == 1:
                sums.setdefault(half, []).append(chain_in[way, item])
            elif rank == 0:
                send(way, 8 + half, part(blocks[4], half) + chain_in[way, item])
            else:
                send(way, item, part(blocks[item // 2], half) + chain_in[way, item])

        for item in range(4, 8):
            for way, rank in ranks(here):
                if rank == 0:
                    send(way, item, part(chain_blocks(way)[item // 2], item % 2))
        events = [(9.5, 2, after_outer), (15.5, 3, after_inner), (21.0, 4, after_spread)]
        for way, rank in ranks(here):
            for item, time in timetable(rank).items():
                events.append((time, way, functools.partial(arrive, way, rank, item)))
        for _, _, action in sorted(events, key=lambda event: event[:2]):
            action()
        for half in range(2):
            result = part(here, half)
            for term in sums[half]:
                result = result + term
            object_ref[half] = result

    def earlier_sends(here):
        for way, rank in ranks(here):
            if rank < CHIPS - 1:
                for slot in range(2):
                    for cut in range(SUM_CUTS):
                        sum_copy(way, slot, cut, power).wait_send()

    by_chip(chip, earlier_sends)
    probe_pair.wait_send()
    for block in range(8):
        pair_copy(block).wait_send()
    by_chip(chip, chain_events)
    settle(outer)
    for part in range(2):
        for side in range(2):
            tiles_of = result[pl.ds(part * half_tiles + side * PATCH // 8, PATCH // 8)]
            probe_ref[pl.ds(part * PATCH, PATCH), pl.ds(side * 128, 128)] = tiles_of.reshape(PATCH, 128)

    def sends(here):
        for way, rank in ranks(here):
            for item in range(10):
                if item < 4 or rank < stays(item):
                    chain_copy(way, item).wait_send()

    by_chip(chip, sends)
    for stage in inner + outer:
        if stage[1] > 1:
            all_of(stage, 0).wait_send()
            all_of(stage, 1).wait_send()


def hand_out(object_in, probe_in, object_ref, probe_ref):
    object_ref[...] = object_in[...]
    probe_ref[...] = probe_in[...]


def chain_blocks(way):
    return ((5, 4, 3, 2, 1), (6, 7, 0, 1, 2))[way]


def stays(item):
    return 5 - item // 2


def timetable(rank, step=2.05):
    spill = {}
    for _ in range(2):
        ready = [{item: 0.0 for item in range(8)}]
        if spill:
            ready[0].update({8 + half: spill[half] for half in range(2)})
        for at in range(CHIPS):
            clock, arrivals = 0.0, {}
            for item in range(10):
                if item in ready[at] and (item < 4 or at < stays(item)):
                    clock = max(clock, ready[at][item]) + step
                    arrivals[item] = clock + LATENCY
            ready.append(arrivals)
        spill = ready[CHIPS]
    return spill if rank == 0 else ready[rank]


def solution(mesh):
    tiles = mesh.shape["tile"]
    grid_x = 4 if tiles == 64 else 2
    grid_z = tiles // 2 // grid_x
    left, right = dft_tables()
    rows = 2 * PATCH
    tile_count = rows * PATCH // (8 * 128)
    block = (2, 32, WIDTH)
    dma = pltpu.SemaphoreType.DMA

    def body(object_field, probe_modes, measured, offsets, counts):
        object_rows, probe = pl.pallas_call(
            functools.partial(kernel, tiles, grid_x, grid_z),
            out_shape=(jax.ShapeDtypeStruct(block, F32), jax.ShapeDtypeStruct((rows, PATCH), F32)),
            in_specs=[ANY, ANY, VMEM, SMEM, SMEM, ANY, ANY],
            out_specs=(VMEM, VMEM),
            scratch_shapes=[
                pltpu.VMEM((2, 2 * STRIP, WIDTH), F32),
                pltpu.VMEM((PAIR, 2, PATCH, PATCH), F32),
                pltpu.VMEM(left.shape, BF16),
                pltpu.VMEM(right.shape, BF16),
                pltpu.VMEM((2, 2, PATCH, PATCH), F32),
                pltpu.VMEM((2, PAIR, 2, PATCH, PATCH), F32),
                pltpu.VMEM((2, PATCH, PATCH), F32),
                pltpu.VMEM((2, 2, PATCH, PATCH), F32),
                pltpu.VMEM((2, 2, PATCH, PATCH), F32),
                pltpu.VMEM((WIDTH, 2 * PATCH), BF16),
                pltpu.VMEM((2, PATCH, 4 * STRIP), BF16),
                pltpu.VMEM((2, PATCH, WIDTH), BF16),
                pltpu.VMEM((2 * STRIP, 4 * PATCH), BF16),
                pltpu.VMEM((2, 4 * STRIP, 2 * PATCH), BF16),
                pltpu.VMEM((2, 4 * PATCH, WIDTH), BF16),
                pltpu.VMEM((2, 16, 32, WIDTH), F32),
                pltpu.VMEM((PAIR, rows, PATCH), F32),
                pltpu.VMEM((2, 8, 32, WIDTH), F32),
                pltpu.VMEM((2, 10, 32, WIDTH), F32),
                pltpu.VMEM((2, 10, 32, WIDTH), F32),
                pltpu.VMEM((rows, PATCH), F32),
                pltpu.VMEM((tile_count, 8, 128), F32),
                pltpu.VMEM((tile_count, 8, 128), F32),
                pltpu.VMEM((grid_x, tile_count // 2 // grid_x, 8, 128), F32),
                pltpu.VMEM((grid_z, tile_count // 2 // grid_z, 8, 128), F32),
                pltpu.VMEM((2 * grid_z, tile_count // 4 // grid_x // grid_z, 8, 128), F32),
                pltpu.VMEM((2 * grid_x, tile_count // 4 // grid_x // grid_z, 8, 128), F32),
                dma((4,)),
                dma, dma,
                dma((2, HALO_CUTS)), dma((2, HALO_CUTS)),
                dma, dma,
                dma((2, 2 * SUM_CUTS)), dma((2, 2 * SUM_CUTS)),
                dma((8,)), dma((8,)),
                dma((2, 10)), dma((2, 10)),
                dma, dma,
                dma((2,)), dma((2,)),
                dma((2,)), dma((2,)),
                dma((2,)), dma((2,)),
                dma((2,)), dma((2,)),
            ],
            compiler_params=pltpu.CompilerParams(collective_id=0, has_side_effects=True, vmem_limit_bytes=LIMIT),
            name="ptychography",
        )(object_field, probe_modes, measured, offsets.T, counts, jnp.asarray(left), jnp.asarray(right))
        object_rows, probe = pl.pallas_call(
            hand_out,
            out_shape=(jax.ShapeDtypeStruct(block, F32), jax.ShapeDtypeStruct((rows, PATCH), F32)),
            in_specs=[VMEM, VMEM],
            out_specs=(VMEM, VMEM),
            compiler_params=pltpu.CompilerParams(vmem_limit_bytes=4 * 1024 * 1024),
            name="hand_out",
        )(object_rows, probe)
        return object_rows, probe.reshape(1, 2, PATCH, PATCH)

    return jax.shard_map(
        body,
        mesh=mesh,
        in_specs=(
            P(None, "tile", None),
            P("mode", None, None, None),
            P("tile", None, None),
            P("tile", None),
            P("tile"),
        ),
        out_specs=(P(None, ("tile", "mode"), None), P("mode", None, None, None)),
        check_vma=False,
    )
```

```python
import functools
import math

import jax
import jax.numpy as jnp
import numpy as np
from jax import lax
from jax.experimental import pallas as pl
from jax.experimental.pallas import tpu as pltpu
from jax.sharding import PartitionSpec as P

MESH = pl.DeviceIdType.MESH
F32 = jnp.float32
BF16 = jnp.bfloat16
VMEM = pl.BlockSpec(memory_space=pltpu.VMEM)
SMEM = pl.BlockSpec(memory_space=pltpu.SMEM)
ANY = pl.BlockSpec(memory_space=pl.ANY)
LIMIT = 56 * 1024 * 1024
PATCH = 256
STRIP = 256
WIDTH = 768
CAP = 4
CHIPS = 4
PAIR = 2

HALO_CUTS = 8
SUM_CUTS = 8
LATENCY = 2.3


def split(value):
    high = value.astype(BF16)
    return high, (value - high.astype(F32)).astype(BF16)


def dft_tables():
    index = np.arange(PATCH)
    angle = 2.0 * math.pi * ((index[:, None] * index[None, :]) % PATCH) / PATCH
    cos, sine = np.cos(angle) / math.sqrt(PATCH), -np.sin(angle) / math.sqrt(PATCH)

    def parts(block):
        high = block.astype(jnp.bfloat16)
        low = (block - high.astype(np.float64)).astype(jnp.bfloat16)
        return high, low

    high, low = parts(np.block([[cos, -sine], [sine, cos]]))
    left = np.concatenate([high, high, low], axis=1)
    high, low = parts(np.block([[cos, sine], [-sine, cos]]))
    right = np.concatenate([high, high, low], axis=0)
    return left, right


def transform(real, imag, left, right):
    high, low = split(jnp.concatenate([real, imag], axis=0))
    mid = jnp.dot(left[...], jnp.concatenate([high, low, high], axis=0), preferred_element_type=F32)
    high, low = split(jnp.concatenate([mid[:PATCH], mid[PATCH:]], axis=1))
    out = jnp.dot(jnp.concatenate([high, low, high], axis=1), right[...], preferred_element_type=F32)
    return out[:, :PATCH], out[:, PATCH:]


def selector(shape, source, target, offset):
    index = lax.broadcasted_iota(jnp.int32, shape, source) - lax.broadcasted_iota(jnp.int32, shape, target)
    return jnp.where(index == offset, 1.0, 0.0).astype(BF16)


def select(left, right):
    return jnp.dot(left, right, preferred_element_type=F32)


def remote(source, target, send_sem, recv_sem, device):
    return pltpu.make_async_remote_copy(
        src_ref=source, dst_ref=target, send_sem=send_sem, recv_sem=recv_sem, device_id=device, device_id_type=MESH
    )


def by_chip(chip, action):
    for here in range(CHIPS):
        pl.when(chip == here)(functools.partial(action, here))


def ranks(here):
    return ((0, here), (1, CHIPS - 1 - here))


def kernel(tiles, grid_x, grid_z, object_hbm, probe_hbm, measured_hbm, offsets_ref, counts_ref, left_hbm, right_hbm,
           object_ref, probe_ref,
           ext, modes, measured, left, right, windows, far, power, staged, arrived, cut_columns,
           cut_rows, put_columns, put_rows, strips, moved, acc, terms, pair_buf, chain_out,
           chain_in, probe_buf, mine, result, x_in, z_in, h_in, local_sem, swap_send, swap_recv, halo_send, halo_recv, cross_send,
           cross_recv, sum_send, sum_recv, pair_send, pair_recv, chain_send, chain_recv, probe_send, probe_recv, x_send,
           x_recv, z_send, z_recv, h_send, h_recv):
    tile, mode = lax.axis_index("tile"), lax.axis_index("mode")
    chip, core = mode // 2, mode % 2
    high, plane = tile % 2, tile // 2
    at_z, at_x = plane % grid_z, plane // grid_z
    after, before = lax.rem(tile + 1, tiles), lax.rem(tile + tiles - 1, tiles)
    sibling = (tile, mode + 1 - 2 * core)
    above = jnp.where(chip < 3, mode + 2, core)
    below = jnp.where(chip > 0, mode - 2, core + 6)
    next_above, last_above = (jnp.where(chip < 3, tile, after), above), (jnp.where(chip < 3, tile, before), above)
    next_below, last_below = (jnp.where(chip > 0, tile, after), below), (jnp.where(chip > 0, tile, before), below)

    def at(x, z, h):
        return ((x * grid_z + z) * 2 + h, mode)

    own_copy = pltpu.make_async_copy(object_hbm, ext.at[:, pl.ds(0, STRIP)], local_sem.at[0])
    probe_copy = pltpu.make_async_copy(probe_hbm.at[0], modes.at[core], local_sem.at[1])
    left_copy = pltpu.make_async_copy(left_hbm, left, local_sem.at[2])
    right_copy = pltpu.make_async_copy(right_hbm, right, local_sem.at[3])
    measured_copy = pltpu.make_async_copy(measured_hbm.at[pl.ds(2 * core, 2)], measured, local_sem.at[4])
    for copy in (own_copy, probe_copy, left_copy, right_copy, measured_copy):
        copy.start()
    barrier = pltpu.get_barrier_semaphore()
    friends = [next_above, last_above, next_below, last_below, sibling]
    friends += [at(lax.rem(at_x + step, grid_x), at_z, high) for step in range(1, grid_x)]
    friends += [at(at_x, lax.rem(at_z + step, grid_z), high) for step in range(1, grid_z)]
    friends += [at(at_x, at_z, 1 - high)]
    for device in friends:
        pl.semaphore_signal(barrier, inc=1, device_id=device, device_id_type=MESH)
    pl.semaphore_wait(barrier, len(friends))

    swap = remote(probe_hbm.at[0], modes.at[core], swap_send, swap_recv, sibling)
    depth = STRIP // 4 // HALO_CUTS
    down_first = (last_below, last_above)

    def halo_rows(way, cut, owner):
        return (2 * way + owner) * (STRIP // 4) + cut * depth

    def halo_copy(way, cut, base):
        row = halo_rows(way, cut, core)
        return remote(
            ext.at[:, pl.ds(base + row, depth)],
            ext.at[:, pl.ds(STRIP + row, depth)],
            halo_send.at[way, cut],
            halo_recv.at[way, cut],
            down_first[way],
        )

    def cross_copy(way, cut, owner):
        block = ext.at[:, pl.ds(STRIP + halo_rows(way, cut, owner), depth)]
        return remote(block, block, cross_send, cross_recv, sibling)

    own_copy.wait()
    for way, last in ((0, 0), (1, 3)):
        @pl.when(chip == last)
        def _():
            for cut in range(HALO_CUTS):
                halo_copy(way, cut, 0).start()
    swap.start()
    for slot in range(2):
        row, column = offsets_ref[0, 2 * core + slot], offsets_ref[1, 2 * core + slot]
        own = pl.ds(slot * PATCH, PATCH)
        cut_columns[:, own] = selector((WIDTH, PATCH), 0, 1, column)
        put_columns[slot] = selector((PATCH, WIDTH), 1, 0, column)
        for copy in range(2):
            cut_rows[slot, :, pl.ds(copy * 2 * STRIP, 2 * STRIP)] = selector((PATCH, 2 * STRIP), 1, 0, row)
            put_rows[:, pl.ds((2 * copy + slot) * PATCH, PATCH)] = selector((2 * STRIP, PATCH), 0, 1, row)

    def cut_strip(part, first, depth):
        for index, value in enumerate(split(ext[part, pl.ds(first, depth)])):
            strips[part, pl.ds(index * 2 * STRIP + first, depth)] = select(value, cut_columns[...]).astype(BF16)

    def halo_events(here):
        step = 8.0 / HALO_CUTS
        events = []
        for way, rank in ((0, CHIPS - 1 - here), (1, here)):
            for cut in range(HALO_CUTS):
                events.append(((rank + 1) * (step + LATENCY) + cut * step, way, cut, rank < CHIPS - 1))
        for index, (_, way, cut, forwards) in enumerate(sorted(events)):
            halo_copy(way, cut, 0).wait_recv()
            if forwards:
                halo_copy(way, cut, STRIP).start()
            cross_copy(way, cut, core).start()
            if index in (1, 4, 7, 10):
                piece = (1, 4, 7, 10).index(index)
                cut_strip(piece // 2, piece % 2 * 128, 128)

    by_chip(chip, halo_events)
    probe_copy.wait()
    swap.wait_recv()
    left_copy.wait()
    right_copy.wait()
    measured_copy.wait()
    crossed = ext.at[:, pl.ds(STRIP, STRIP // 2)]
    all_across = remote(crossed, crossed, cross_send, cross_recv, sibling)
    all_across.wait_recv()

    sum_depth = PATCH // SUM_CUTS

    def sum_copy(way, slot, cut, source):
        rows = pl.ds(cut * sum_depth, sum_depth)
        item = slot * SUM_CUTS + cut
        return remote(
            source.at[slot, rows],
            arrived.at[way, slot, rows],
            sum_send.at[way, item],
            sum_recv.at[way, item],
            ((tile, mode + 2), (tile, mode - 2))[way],
        )

    def forward(slot):
        window = []
        for part in range(2):
            block = select(cut_rows[slot], strips[part, :, pl.ds(slot * PATCH, PATCH)])
            windows[slot, part] = block
            window.append(block)
        for pair in range(PAIR):
            mode_real, mode_imag = modes[pair, 0], modes[pair, 1]
            far_real, far_imag = transform(
                mode_real * window[0] - mode_imag * window[1],
                mode_real * window[1] + mode_imag * window[0],
                left,
                right,
            )
            far[slot, pair, 0] = far_real
            far[slot, pair, 1] = far_imag
            if pair == 0:
                power[slot] = far_real * far_real + far_imag * far_imag
            else:
                power[slot] += far_real * far_real + far_imag * far_imag

    def first_sums(slot):
        for way, first in ((0, 0), (1, 3)):
            @pl.when(chip == first)
            def _():
                for cut in range(SUM_CUTS):
                    sum_copy(way, slot, cut, power).start()

    for part in range(2):
        cut_strip(part, STRIP, STRIP)
    for slot in range(2):
        forward(slot)
        first_sums(slot)

    def sum_events(late, here):
        step = 5.3 / SUM_CUTS
        events = []
        for way, rank in ranks(here):
            if rank > 0:
                for slot in range(2):
                    for cut in range(SUM_CUTS):
                        time = rank * (step + LATENCY) + (slot * SUM_CUTS + cut) * step
                        events.append((time, way, slot, cut, rank < CHIPS - 1))
        for _, way, slot, cut, forwards in sorted(events):
            if late != (not forwards and slot == 1):
                continue
            sum_copy(way, slot, cut, power).wait_recv()
            if forwards:
                rows = pl.ds(cut * sum_depth, sum_depth)
                staged[way, slot, rows] = power[slot, rows] + arrived[way, slot, rows]
                sum_copy(way, slot, cut, staged.at[way]).start()

    def intensity(slot):
        lower = jnp.where(chip > 0, arrived[0, slot], 0.0)
        upper = jnp.where(chip < 3, arrived[1, slot], 0.0)
        return power[slot] + (lower + upper)

    def backward(slot):
        index = 2 * core + slot
        amplitude = jnp.sqrt(measured[slot].astype(F32))
        live = (index < counts_ref[0]).astype(F32)
        scaling = live * (1.0 - amplitude / jnp.sqrt(jnp.maximum(intensity(slot), 1.0)))
        win_real, win_imag = windows[slot, 0], windows[slot, 1]
        sums = None
        for pair in (1 - core, core):
            back_real, minus_imag = transform(
                scaling * far[slot, pair, 0], -(scaling * far[slot, pair, 1]), left, right
            )
            mode_real, mode_imag = modes[pair, 0], modes[pair, 1]
            grads = (
                mode_real * back_real - mode_imag * minus_imag,
                -(mode_real * minus_imag + mode_imag * back_real),
            )
            sums = grads if sums is None else (sums[0] + grads[0], sums[1] + grads[1])
            probe_real = win_real * back_real - win_imag * minus_imag
            probe_imag = -(win_real * minus_imag + win_imag * back_real)
            if slot == 0:
                terms[pair, pl.ds(0, PATCH)] = probe_real
                terms[pair, pl.ds(PATCH, PATCH)] = probe_imag
            else:
                terms[pair, pl.ds(0, PATCH)] += probe_real
                terms[pair, pl.ds(PATCH, PATCH)] += probe_imag
                if pair is not core:
                    probe_pair.start()
        return sums

    def place(slot, sums):
        for part, term in enumerate(sums):
            for copy, value in enumerate(split(term)):
                rows = pl.ds((2 * copy + slot) * PATCH, PATCH)
                moved[part, rows] = select(value, put_columns[slot]).astype(BF16)

    probe_pair = remote(terms.at[1 - core], probe_buf, probe_send, probe_recv, sibling)
    swap.wait_send()
    all_across.wait_send()
    for cut in range(HALO_CUTS):
        for way in range(2):
            halo_copy(way, cut, 0).wait_send()
    by_chip(chip, functools.partial(sum_events, False))
    place(0, backward(0))
    by_chip(chip, functools.partial(sum_events, True))
    sums = backward(1)

    def pair_copy(block):
        return remote(
            acc.at[:, 2 * block + 1 - core], pair_buf.at[:, block], pair_send.at[block], pair_recv.at[block], sibling
        )

    def put(first, blocks):
        for half in range(2):
            total = select(put_rows[pl.ds(first, STRIP)], moved[half])
            for index in range(8):
                acc[half, first // 32 + index] = total[32 * index : 32 * index + 32]
        for block in blocks:
            pair_copy(block).start()

    def group_x(index):
        return at(index, at_z, high)

    def group_z(index):
        return at(at_x, index, high)

    x_tiles = mine.shape[0] // grid_x
    z_tiles = x_tiles // grid_z
    over_x = ((group_x, grid_x, at_x, 0, x_tiles, x_in, x_send, x_recv),)
    over_z = ((group_z, grid_z, at_z, at_x * x_tiles, z_tiles, z_in, z_send, z_recv),)
    own_tiles = pl.ds(at_x * x_tiles + at_z * z_tiles, z_tiles)
    h_copy = remote(mine.at[own_tiles], h_in, h_send, h_recv, at(at_x, at_z, 1 - high))

    def scatter_copy(stage, step):
        group, count, here, base, depth, inbox, send, recv = stage
        peer = lax.rem(here + step + 1, count)
        return remote(mine.at[pl.ds(base + peer * depth, depth)], inbox.at[step], send.at[0], recv.at[0], group(peer))

    def back_copy(stage, step):
        group, count, here, base, depth, inbox, send, recv = stage
        rows = result.at[pl.ds(base + here * depth, depth)]
        return remote(rows, rows, send.at[1], recv.at[1], group(lax.rem(here + step + 1, count)))

    def all_of(stage, turn):
        group, count, here, base, depth, inbox, send, recv = stage
        if turn == 0:
            block = inbox.at[pl.ds(0, count - 1)]
        else:
            block = result.at[pl.ds(0, (count - 1) * depth)]
        return remote(block, block, send.at[turn], recv.at[turn], sibling)

    def steps(stages):
        order = [(min(step + 1, stage[1] - step - 1), step, stage) for stage in stages for step in range(stage[1] - 1)]
        return [(stage, step) for _, step, stage in sorted(order, key=lambda entry: entry[:2])]

    def scatter(stages):
        for stage, step in steps(stages):
            scatter_copy(stage, step).start()

    def collect(stages, target):
        for stage in stages:
            if stage[1] > 1:
                all_of(stage, 0).wait_recv()
            group, count, here, base, depth, inbox, send, recv = stage
            rows = pl.ds(base + here * depth, depth)
            total = mine[rows]
            for step in range(count - 1):
                total = total + inbox[step]
            target[rows] = total

    def spread(stages):
        for stage, step in steps(stages):
            back_copy(stage, step).start()

    def settle(stages):
        for stage in stages:
            if stage[1] > 1:
                all_of(stage, 1).wait_recv()

    def after_x():
        collect(over_x, mine)
        scatter(over_z)

    def after_z():
        collect(over_z, mine)
        h_copy.start()

    def after_h():
        h_copy.wait_recv()
        result[own_tiles] = mine[own_tiles] + h_in[...]
        spread(over_z)

    def after_z_back():
        settle(over_z)
        spread(over_x)

    probe_pair.wait_recv()
    for part in range(2):
        rows = pl.ds(part * PATCH, PATCH)
        total = probe_buf[rows] + terms[core, rows]
        for side in range(2):
            tiles_of = total[:, side * 128 : side * 128 + 128].reshape(PATCH // 8, 8, 128)
            mine[pl.ds(part * mine.shape[0] // 2 + side * PATCH // 8, PATCH // 8)] = tiles_of
    scatter(over_x)
    place(1, sums)
    put(STRIP, (5, 6, 4, 7))

    def chain_copy(way, item):
        return remote(
            chain_out.at[way, item], chain_in.at[way, item], chain_send.at[way, item], chain_recv.at[way, item],
            (next_above, next_below)[way],
        )

    def first_rows(here):
        for item in range(4):
            for way, rank in ranks(here):
                if rank == 0:
                    block, half = chain_blocks(way)[item // 2], item % 2
                    if half == 0:
                        pair_copy(block).wait_recv()
                    chain_out[way, item] = pair_buf[half, block] + acc[half, 2 * block + core]
                    chain_copy(way, item).start()

    by_chip(chip, first_rows)
    put(0, (3, 0, 2, 1))

    def chain_events(here):
        ready = {block for way, rank in ranks(here) if rank == 0 for block in chain_blocks(way)[:2]}

        def part(block, half):
            if block not in ready:
                ready.add(block)
                pair_copy(block).wait_recv()
            return pair_buf[half, block] + acc[half, 2 * block + core]

        def send(way, item, value):
            chain_out[way, item] = value
            chain_copy(way, item).start()

        sums = {}

        def arrive(way, rank, item):
            chain_copy(way, item).wait_recv()
            blocks, half = chain_blocks(way), item % 2
            if item >= 4 and stays(item) == rank or rank == 0 and item // 2 == 1:
                sums.setdefault(half, []).append(chain_in[way, item])
            elif rank == 0:
                send(way, 8 + half, part(blocks[4], half) + chain_in[way, item])
            else:
                send(way, item, part(blocks[item // 2], half) + chain_in[way, item])

        for item in range(4, 8):
            for way, rank in ranks(here):
                if rank == 0:
                    send(way, item, part(chain_blocks(way)[item // 2], item % 2))
        events = [(8.0, 2, after_x), (14.0, 3, after_z), (17.0, 4, after_h), (23.0, 5, after_z_back)]
        for way, rank in ranks(here):
            for item, time in timetable(rank).items():
                events.append((time, way, functools.partial(arrive, way, rank, item)))
        for _, _, action in sorted(events, key=lambda event: event[:2]):
            action()
        for half in range(2):
            result = part(here, half)
            for term in sums[half]:
                result = result + term
            object_ref[half] = result

    def earlier_sends(here):
        for way, rank in ranks(here):
            if rank < CHIPS - 1:
                for slot in range(2):
                    for cut in range(SUM_CUTS):
                        sum_copy(way, slot, cut, power).wait_send()

    by_chip(chip, earlier_sends)
    probe_pair.wait_send()
    for block in range(8):
        pair_copy(block).wait_send()
    by_chip(chip, chain_events)
    def sends(here):
        for way, rank in ranks(here):
            for item in range(10):
                if item < 4 or rank < stays(item):
                    chain_copy(way, item).wait_send()

    by_chip(chip, sends)
    h_copy.wait_send()
    settle(over_x)
    for part in range(2):
        for side in range(2):
            tiles_of = result[pl.ds(part * mine.shape[0] // 2 + side * PATCH // 8, PATCH // 8)]
            probe_ref[pl.ds(part * PATCH, PATCH), pl.ds(side * 128, 128)] = tiles_of.reshape(PATCH, 128)
    for stage in over_z + over_x:
        if stage[1] > 1:
            all_of(stage, 0).wait_send()
            all_of(stage, 1).wait_send()


def hand_out(object_in, probe_in, object_ref, probe_ref):
    object_ref[...] = object_in[...]
    probe_ref[...] = probe_in[...]


def chain_blocks(way):
    return ((5, 4, 3, 2, 1), (6, 7, 0, 1, 2))[way]


def stays(item):
    return 5 - item // 2


def timetable(rank, step=2.05):
    spill = {}
    for _ in range(2):
        ready = [{item: 0.0 for item in range(8)}]
        if spill:
            ready[0].update({8 + half: spill[half] for half in range(2)})
        for at in range(CHIPS):
            clock, arrivals = 0.0, {}
            for item in range(10):
                if item in ready[at] and (item < 4 or at < stays(item)):
                    clock = max(clock, ready[at][item]) + step
                    arrivals[item] = clock + LATENCY
            ready.append(arrivals)
        spill = ready[CHIPS]
    return spill if rank == 0 else ready[rank]


def solution(mesh):
    tiles = mesh.shape["tile"]
    grid_x = 4 if tiles == 64 else 2
    grid_z = tiles // 2 // grid_x
    left, right = dft_tables()
    rows = 2 * PATCH
    tile_count = rows * PATCH // (8 * 128)
    block = (2, 32, WIDTH)
    dma = pltpu.SemaphoreType.DMA

    def body(object_field, probe_modes, measured, offsets, counts):
        object_rows, probe = pl.pallas_call(
            functools.partial(kernel, tiles, grid_x, grid_z),
            out_shape=(jax.ShapeDtypeStruct(block, F32), jax.ShapeDtypeStruct((rows, PATCH), F32)),
            in_specs=[ANY, ANY, ANY, SMEM, SMEM, ANY, ANY],
            out_specs=(VMEM, VMEM),
            scratch_shapes=[
                pltpu.VMEM((2, 2 * STRIP, WIDTH), F32),
                pltpu.VMEM((PAIR, 2, PATCH, PATCH), F32),
                pltpu.VMEM((2, PATCH, PATCH), BF16),
                pltpu.VMEM(left.shape, BF16),
                pltpu.VMEM(right.shape, BF16),
                pltpu.VMEM((2, 2, PATCH, PATCH), F32),
                pltpu.VMEM((2, PAIR, 2, PATCH, PATCH), F32),
                pltpu.VMEM((2, PATCH, PATCH), F32),
                pltpu.VMEM((2, 2, PATCH, PATCH), F32),
                pltpu.VMEM((2, 2, PATCH, PATCH), F32),
                pltpu.VMEM((WIDTH, 2 * PATCH), BF16),
                pltpu.VMEM((2, PATCH, 4 * STRIP), BF16),
                pltpu.VMEM((2, PATCH, WIDTH), BF16),
                pltpu.VMEM((2 * STRIP, 4 * PATCH), BF16),
                pltpu.VMEM((2, 4 * STRIP, 2 * PATCH), BF16),
                pltpu.VMEM((2, 4 * PATCH, WIDTH), BF16),
                pltpu.VMEM((2, 16, 32, WIDTH), F32),
                pltpu.VMEM((PAIR, rows, PATCH), F32),
                pltpu.VMEM((2, 8, 32, WIDTH), F32),
                pltpu.VMEM((2, 10, 32, WIDTH), F32),
                pltpu.VMEM((2, 10, 32, WIDTH), F32),
                pltpu.VMEM((rows, PATCH), F32),
                pltpu.VMEM((tile_count, 8, 128), F32),
                pltpu.VMEM((tile_count, 8, 128), F32),
                pltpu.VMEM((grid_x, tile_count // grid_x, 8, 128), F32),
                pltpu.VMEM((grid_z, tile_count // grid_x // grid_z, 8, 128), F32),
                pltpu.VMEM((tile_count // grid_x // grid_z, 8, 128), F32),
                dma((5,)),
                dma, dma,
                dma((2, HALO_CUTS)), dma((2, HALO_CUTS)),
                dma, dma,
                dma((2, 2 * SUM_CUTS)), dma((2, 2 * SUM_CUTS)),
                dma((8,)), dma((8,)),
                dma((2, 10)), dma((2, 10)),
                dma, dma,
                dma((2,)), dma((2,)),
                dma((2,)), dma((2,)),
                dma, dma,
            ],
            compiler_params=pltpu.CompilerParams(collective_id=0, has_side_effects=True, vmem_limit_bytes=LIMIT),
            name="ptychography",
        )(object_field, probe_modes, measured, offsets.T, counts, jnp.asarray(left), jnp.asarray(right))
        object_rows, probe = pl.pallas_call(
            hand_out,
            out_shape=(jax.ShapeDtypeStruct(block, F32), jax.ShapeDtypeStruct((rows, PATCH), F32)),
            in_specs=[VMEM, VMEM],
            out_specs=(VMEM, VMEM),
            compiler_params=pltpu.CompilerParams(vmem_limit_bytes=LIMIT),
            name="hand_out",
        )(object_rows, probe)
        return object_rows, probe.reshape(1, 2, PATCH, PATCH)

    return jax.shard_map(
        body,
        mesh=mesh,
        in_specs=(
            P(None, "tile", None),
            P("mode", None, None, None),
            P("tile", None, None),
            P("tile", None),
            P("tile"),
        ),
        out_specs=(P(None, ("tile", "mode"), None), P("mode", None, None, None)),
        check_vma=False,
    )
```
